256 devices in a mesh: slide: 8 (over x, core), seq: 32 (over y, z).
Axes of the slice: x: 4, y: 4, z: 8, core: 2. Of those that a mesh axis runs over, the one named last changes fastest.
Arguments:
- queries: bfloat16 [8, 8192, 1536], P('slide', 'seq'), may hold values from -9 to 9
- key_rows: bfloat16 [8, 8192, 1536], P('slide', 'seq'), may hold values from -9 to 9
- value_rows: bfloat16 [8, 8192, 1536], P('slide', 'seq'), may hold values from -12 to 12
- tissue: int32 [8, 8192], P('slide', 'seq'), may hold values from 0 to 1, as said below
- segment_len: int32 [24], replicated, may hold values from 128 to 256, as said below
- dilation: int32 [24], replicated, may hold values from 1 to 4, as said below
- out_weight: bfloat16 [1536, 1536], P(('slide', 'seq')), may hold values from -0.15625 to 0.15625
- grad_out: bfloat16 [8, 8192, 1536], P('slide', 'seq'), may hold values from -6 to 6
Outputs:
- layer_out: bfloat16 [8, 8192, 1536], P('slide', 'seq')
- grad_query: bfloat16 [8, 8192, 1536], P('slide', 'seq')
- grad_key: bfloat16 [8, 8192, 1536], P('slide', 'seq')
- grad_value: bfloat16 [8, 8192, 1536], P('slide', 'seq')
- grad_weight: float32 [1536, 1536], P(('slide', 'seq'))
The draws below stay inside these ranges and needn't reach their ends.
Inputs may be any that keep to these rules, and one draw needn't show every extreme that they name: 1 for tissue, 0 for background. `segment_len`: each entry is 256 or 128, and each value is taken by some head. `dilation`: each entry is 1, 2 or 4; some head has 1 and some head 4.
All inputs are finite; a program needn't handle non-finite values.
Results may differ from the reference program's by a relative error of at most 0.0079.
Values may be sent and summed in bfloat16 or wider, within the bound.
A program may use at most 128 MiB of HBM per device.

```python
import math
import jax
import jax.numpy as jnp
from jax import lax

H = 24
HD = 64
TOK_DEV = 256
D = 1536
SLIDES = 8
SEQ_LEN = 8192
RATE = 32


def tissue_map(key):
    own_key = jax.random.fold_in(key, 101)
    key_center, key_span, key_hole = jax.random.split(own_key, 3)
    centers = jax.random.randint(key_center, (SLIDES, 8), 0, SEQ_LEN)
    half_spans = jax.random.randint(key_span, (SLIDES, 8), SEQ_LEN // 32, SEQ_LEN // 8 + 1)
    places = jnp.arange(SEQ_LEN, dtype=jnp.int32)
    inside = jnp.any(jnp.abs(places[None, None, :] - centers[:, :, None]) < half_spans[:, :, None], axis=1)
    hole_mask = jax.random.randint(key_hole, (SLIDES, SEQ_LEN), 0, 8) != 0
    return (inside & hole_mask).astype(jnp.int32)


def draw_queries(key, part):
    own_key = jax.random.fold_in(key, 1)
    array_shape = (SLIDES, SEQ_LEN, D)
    return (1.5 * jax.random.truncated_normal(own_key, -6.0, 6.0, array_shape, jnp.float32)).astype(jnp.bfloat16)


def draw_key_rows(key, part):
    own_key = jax.random.fold_in(key, 2)
    array_shape = (SLIDES, SEQ_LEN, D)
    return (1.5 * jax.random.truncated_normal(own_key, -6.0, 6.0, array_shape, jnp.float32)).astype(jnp.bfloat16)


def draw_tissue(key, part):
    return tissue_map(key)


def draw_segment_len(key, part):
    own_key = jax.random.fold_in(key, 3)
    key_level, key_first, key_step = jax.random.split(own_key, 3)
    halves = jax.random.randint(key_level, (H,), 0, 2)
    first_head = jax.random.randint(key_first, (), 0, H)
    second_head = (first_head + jax.random.randint(key_step, (), 1, H)) % H
    heads_idx = jnp.arange(H, dtype=jnp.int32)
    halves = jnp.where(heads_idx == first_head, 0, jnp.where(heads_idx == second_head, 1, halves))
    return (TOK_DEV // (1 + halves)).astype(jnp.int32)


def draw_dilation(key, part):
    own_key = jax.random.fold_in(key, 4)
    key_level, key_first, key_step = jax.random.split(own_key, 3)
    powers = jax.random.randint(key_level, (H,), 0, 3)
    first_head = jax.random.randint(key_first, (), 0, H)
    second_head = (first_head + jax.random.randint(key_step, (), 1, H)) % H
    heads_idx = jnp.arange(H, dtype=jnp.int32)
    powers = jnp.where(heads_idx == first_head, 2, jnp.where(heads_idx == second_head, 0, powers))
    return jnp.where(powers == 0, 1, jnp.where(powers == 1, 2, 4)).astype(jnp.int32)


def shard_levels(stream_key, dims, pieces, least, largest):
    def one(axis_at, shards_of):
        steps = jax.random.uniform(jax.random.fold_in(jax.random.fold_in(stream_key, 6), axis_at), (shards_of,), jnp.float32, least / len(pieces), largest / len(pieces))
        return jnp.repeat(jnp.exp(steps), dims[axis_at] // shards_of).reshape((-1,) + (1,) * (len(dims) - axis_at - 1))

    factor_of = one(*pieces[0])
    for cut in pieces[1:]:
        factor_of = factor_of * one(*cut)
    return factor_of


def scatter_about(stream_key, shape, spread, reach, cuts=(), kind=jnp.bfloat16):
    array = jax.random.normal(stream_key, shape, jnp.float32) * spread
    if len(cuts) > 0:
        array = shard_levels(stream_key, shape, cuts, -0.22, 0.18) * array
    return jnp.clip(array, min=-reach, max=reach).astype(kind)


def setup_inputs(seed: int = 0) -> dict:
    streams_of = jax.random.split(jax.random.key(seed), 9)
    return {
        "queries": draw_queries(jax.random.fold_in(streams_of[8], 71), 0),
        "key_rows": draw_key_rows(jax.random.fold_in(streams_of[8], 71), 0),
        "value_rows": scatter_about(streams_of[2], (SLIDES, SEQ_LEN, D), 2.0, 12.0, ((0, 8), (1, 32))),
        "tissue": draw_tissue(jax.random.fold_in(streams_of[8], 71), 0),
        "segment_len": draw_segment_len(jax.random.fold_in(streams_of[8], 71), 0),
        "dilation": draw_dilation(jax.random.fold_in(streams_of[8], 71), 0),
        "out_weight": scatter_about(streams_of[6], (D, D), D ** -0.5, 0.15625, ((0, 256),)),
        "grad_out": scatter_about(streams_of[7], (SLIDES, SEQ_LEN, D), 1.0, 6.0, ((0, 8), (1, 32))),
    }


def heads_of(matrix):
    return matrix.reshape(matrix.shape[:-1] + (H, HD))

def local_allowed(keep_row, segment_len, dilation):
    count = keep_row.shape[0]
    places = jnp.arange(count, dtype=jnp.int32)
    seg_col = segment_len.astype(jnp.int32)[:, None, None]
    rate_col = dilation.astype(jnp.int32)[:, None, None]
    row_pos = places[None, :, None]
    col_pos = places[None, None, :]
    inside = (row_pos // seg_col == col_pos // seg_col) & (row_pos % rate_col == col_pos % rate_col)
    inside = inside & (keep_row[None, None, :] == 1)
    return inside | (row_pos == col_pos)

def scores_of(q_heads, k_heads):
    return jnp.einsum('ihd,jhd->hij', q_heads.astype(jnp.float32), k_heads.astype(jnp.float32)) * HD ** (-0.5)

def forward_part(q_heads, k_heads, v_heads, allowed):
    scores = scores_of(q_heads, k_heads)
    top_all = lax.optimization_barrier(jnp.max(jnp.where(allowed, scores, -1e+30), axis=2))
    weights = jnp.where(allowed, jnp.exp(scores - top_all[:, :, None]), 0.0)
    totals = lax.optimization_barrier(jnp.sum(weights, axis=2))
    rounded = lax.optimization_barrier(weights.astype(jnp.bfloat16)).astype(jnp.float32)
    summed = jnp.einsum('hij,jhd->ihd', rounded, v_heads.astype(jnp.float32))
    return (top_all, totals, summed)

def backward_part(q_heads, k_heads, v_heads, allowed, lse, delta, d_heads):
    scale = HD ** (-0.5)
    scores = scores_of(q_heads, k_heads)
    probs = jnp.where(allowed, jnp.exp(scores - lse[:, :, None]), 0.0)
    probs_low = lax.optimization_barrier(probs.astype(jnp.bfloat16)).astype(jnp.float32)
    d_float = d_heads.astype(jnp.float32)
    grad_v = jnp.einsum('hij,ihd->jhd', probs_low, d_float)
    dprob = jnp.einsum('ihd,jhd->hij', d_float, v_heads.astype(jnp.float32))
    dscore = probs * (dprob - delta[:, :, None])
    dscore = lax.optimization_barrier(dscore.astype(jnp.bfloat16)).astype(jnp.float32)
    grad_q = jnp.einsum('hij,jhd->ihd', dscore, k_heads.astype(jnp.float32)) * scale
    grad_k = jnp.einsum('hij,ihd->jhd', dscore, q_heads.astype(jnp.float32)) * scale
    return (grad_q, grad_k, grad_v)

def rounded_far(matrix):
    return lax.optimization_barrier(matrix.astype(jnp.bfloat16)).astype(jnp.float32)

def reference(queries, key_rows, value_rows, tissue, segment_len, dilation, out_weight, grad_out):

    def one_slide(carry, items):
        q_rows, k_rows, v_rows, keep_row, upstream = items
        length = q_rows.shape[0]
        blocks = length // TOK_DEV
        far_rows = length // RATE

        def to_near(matrix):
            return matrix.reshape((blocks, TOK_DEV) + matrix.shape[1:])

        def to_far(matrix):
            return jnp.swapaxes(matrix.reshape((far_rows, RATE) + matrix.shape[1:]), 0, 1)

        def from_far(matrix):
            return jnp.swapaxes(matrix, 0, 1).reshape((length,) + matrix.shape[2:])

        def near_stats(stats):
            return jnp.transpose(stats, (1, 0, 2)).reshape(H, length)

        def far_stats(stats):
            return jnp.transpose(stats, (1, 2, 0)).reshape(H, length)

        def stats_near(stats):
            return jnp.transpose(stats.reshape(H, blocks, TOK_DEV), (1, 0, 2))

        def stats_far(stats):
            return jnp.transpose(stats.reshape(H, far_rows, RATE), (2, 0, 1))
        q_heads = heads_of(q_rows)
        k_heads = heads_of(k_rows)
        v_heads = heads_of(v_rows)
        near_mask = jax.vmap(lambda part_keep: local_allowed(part_keep, segment_len, dilation))(to_near(keep_row))
        far_mask = (to_far(keep_row) == 1)[:, None, None, :]
        m_near, l_near, acc_near = jax.vmap(forward_part)(to_near(q_heads), to_near(k_heads), to_near(v_heads), near_mask)
        m_far, l_far, acc_far = jax.vmap(forward_part)(to_far(q_heads), to_far(k_heads), to_far(v_heads), far_mask)
        m_near = near_stats(m_near)
        l_near = near_stats(l_near)
        acc_near = acc_near.reshape(length, H, HD)
        m_far = far_stats(m_far)
        l_far = far_stats(l_far)
        acc_far = from_far(acc_far)
        top_all = jnp.maximum(m_near, m_far)
        scale_near = jnp.exp(m_near - top_all)
        scale_far = jnp.exp(m_far - top_all)
        totals = scale_near * l_near + scale_far * l_far
        attn_f = (scale_near.T[:, :, None] * acc_near + scale_far.T[:, :, None] * acc_far) / totals.T[:, :, None]
        lse = top_all + jnp.log(totals)
        attn = attn_f.reshape(length, H * HD).astype(jnp.bfloat16)
        layer_out = jnp.dot(attn, out_weight, preferred_element_type=jnp.float32).astype(jnp.bfloat16)
        d_attn = jnp.dot(upstream, out_weight.T, preferred_element_type=jnp.float32).astype(jnp.bfloat16)
        d_heads = heads_of(d_attn)
        delta = lax.optimization_barrier(jnp.sum(d_heads.astype(jnp.float32) * attn_f, axis=2)).T
        gq_near, gk_near, gv_near = jax.vmap(backward_part)(to_near(q_heads), to_near(k_heads), to_near(v_heads), near_mask, stats_near(lse), stats_near(delta), to_near(d_heads))
        gq_far, gk_far, gv_far = jax.vmap(backward_part)(to_far(q_heads), to_far(k_heads), to_far(v_heads), far_mask, stats_far(lse), stats_far(delta), to_far(d_heads))
        grad_q = gq_near.reshape(length, H * HD) + rounded_far(from_far(gq_far).reshape(length, H * HD))
        grad_k = gk_near.reshape(length, H * HD) + rounded_far(from_far(gk_far).reshape(length, H * HD))
        grad_v = gv_near.reshape(length, H * HD) + rounded_far(from_far(gv_far).reshape(length, H * HD))
        term = lax.dot_general(attn, upstream, (((0,), (0,)), ((), ())), preferred_element_type=jnp.float32)
        outputs = (layer_out, grad_q.astype(jnp.bfloat16), grad_k.astype(jnp.bfloat16), grad_v.astype(jnp.bfloat16))
        return (carry + term, outputs)
    start = jnp.zeros((D, D), jnp.float32)
    total_term, outputs = lax.scan(one_slide, start, (queries, key_rows, value_rows, tissue, grad_out))
    grad_weight = total_term * (1.0 / math.sqrt(SLIDES * SEQ_LEN))
    return (outputs[0], outputs[1], outputs[2], outputs[3], grad_weight)
```

```python
import functools
import math

import jax
import jax.numpy as jnp
from jax import lax
from jax.experimental import pallas as pl
from jax.experimental.pallas import tpu as pltpu
from jax.sharding import PartitionSpec as P

HD = 64
NX, NC, NY, NZ = 4, 2, 4, 8
MESH = pl.DeviceIdType.MESH


def place():
    slide = lax.axis_index("slide")
    seq = lax.axis_index("seq")
    return lax.div(slide, NC), lax.rem(slide, NC), lax.div(seq, NZ), lax.rem(seq, NZ)


def device(x, c, y, z):
    return (x * NC + c, y * NZ + z)


def line_peers(x, c, y, z):
    peers = [device(x, 1 - c, y, z)]
    peers += [device(lax.rem(x + step, NX), c, y, z) for step in range(1, NX)]
    peers += [device(x, c, lax.rem(y + step, NY), z) for step in range(1, NY)]
    peers += [device(x, c, y, lax.rem(z + step, NZ)) for step in range(1, NZ)]
    return peers


def greet(peers):
    barrier = pltpu.get_barrier_semaphore()
    for peer in peers:
        pl.semaphore_signal(barrier, inc=1, device_id=peer, device_id_type=MESH)
    pl.semaphore_wait(barrier, len(peers))


def remote(src, dst, send, recv, peer):
    return pltpu.make_async_remote_copy(
        src_ref=src,
        dst_ref=dst,
        send_sem=send,
        recv_sem=recv,
        device_id=peer,
        device_id_type=MESH,
    )


def gather_kernel(w_ref, full, z_src, z_in, send, z_recv, y_recv, x_recv, c_recv):
    x, c, y, z = place()
    greet(line_peers(x, c, y, z))
    rows, width = w_ref.shape
    z_src[...] = jnp.zeros_like(z_src)
    z_src[0:rows, :] = w_ref[...]
    z_in[z] = z_src[...]
    started = []
    for step in range(1, NZ):
        peer = device(x, c, y, lax.rem(z + step, NZ))
        copy = remote(z_src, z_in.at[z], send.at[len(started)], z_recv.at[step - 1], peer)
        copy.start()
        started.append(copy)
    for step in range(NZ - 1):
        started[step].wait_recv()
    pad = z_src.shape[0]
    out_row = lax.broadcasted_iota(jnp.int32, (NZ * rows, NZ * pad), 0)
    in_row = lax.broadcasted_iota(jnp.int32, (NZ * rows, NZ * pad), 1)
    pick = (in_row == lax.div(out_row, rows) * pad + lax.rem(out_row, rows)).astype(jnp.bfloat16)
    block = NZ * rows
    mine = pl.ds(pl.multiple_of(((x * NC + c) * NY + y) * block, 16), block)
    full[mine, :] = jnp.dot(
        pick, z_in[...].reshape(NZ * pad, width), preferred_element_type=jnp.float32
    ).astype(jnp.bfloat16)
    first = len(started)
    for step in range(1, NY):
        peer = device(x, c, lax.rem(y + step, NY), z)
        copy = remote(full.at[mine], full.at[mine], send.at[len(started)], y_recv.at[step - 1], peer)
        copy.start()
        started.append(copy)
    for copy in started[first:]:
        copy.wait_recv()
    line = NY * block

    def line_of(xx, cc):
        return pl.ds(pl.multiple_of((xx * NC + cc) * line, 16), line)

    first = len(started)
    own = line_of(x, c)
    for step in range(1, NX):
        peer = device(lax.rem(x + step, NX), c, y, z)
        copy = remote(full.at[own], full.at[own], send.at[len(started)], x_recv.at[step - 1], peer)
        copy.start()
        started.append(copy)
    sibling = device(x, 1 - c, y, z)
    last = []
    for step in range(NX):
        if step > 0:
            started[first + step - 1].wait_recv()
        there = line_of(lax.rem(x + NX - step, NX), c)
        copy = remote(full.at[there], full.at[there], send.at[len(started)], c_recv.at[step], sibling)
        copy.start()
        started.append(copy)
        last.append(copy)
    for copy in last:
        copy.wait_recv()
    for copy in started:
        copy.wait_send()


def gather_weight(shard):
    rows, width = shard.shape
    return pl.pallas_call(
        gather_kernel,
        out_shape=jax.ShapeDtypeStruct((rows * NX * NC * NY * NZ, width), shard.dtype),
        in_specs=[pl.BlockSpec(memory_space=pltpu.VMEM)],
        out_specs=pl.BlockSpec(memory_space=pltpu.VMEM),
        scratch_shapes=[
            pltpu.VMEM((16, width), shard.dtype),
            pltpu.VMEM((NZ, 16, width), shard.dtype),
            pltpu.SemaphoreType.DMA((NZ + NY + 2 * NX,)),
            pltpu.SemaphoreType.DMA((NZ,)),
            pltpu.SemaphoreType.DMA((NY,)),
            pltpu.SemaphoreType.DMA((NX,)),
            pltpu.SemaphoreType.DMA((NX,)),
        ],
        compiler_params=pltpu.CompilerParams(
            collective_id=0, has_side_effects=True, vmem_limit_bytes=50 * 1024 * 1024
        ),
    )(shard)


def reduce_kernel(
    factor, part, out, c_in, x_out, x_in, y_out, y_in, z_out, z_in, send, c_recv, x_recv, y_recv, z_recv
):
    x, c, y, z = place()
    greet(line_peers(x, c, y, z))
    line, width = x_out.shape[1:]
    block = line // NY
    rows = block // NZ

    def line_of(xx, cc):
        return pl.ds(pl.multiple_of((xx * NC + cc) * line, 16), line)

    started = []
    sibling = device(x, 1 - c, y, z)
    for step in range(NX):
        to = lax.rem(x + step + 1, NX)
        copy = remote(
            part.at[line_of(to, 1 - c)], c_in.at[step], send.at[len(started)], c_recv.at[step], sibling
        )
        copy.start()
        started.append(copy)
    ahead = []
    for step in range(NX):
        started[step].wait_recv()
        to = lax.rem(x + step + 1, NX)
        x_out[step] = part[line_of(to, c), :] + c_in[step]
        if step < NX - 1:
            copy = remote(
                x_out.at[step], x_in.at[step], send.at[len(started)], x_recv.at[step], device(to, c, y, z)
            )
            copy.start()
            started.append(copy)
            ahead.append(copy)
    for copy in ahead:
        copy.wait_recv()
    total = x_out[NX - 1]
    for step in range(NX - 1):
        total = total + x_in[step]
    y_out[...] = total.reshape(NY, block, width)
    ahead = []
    for step in range(NY - 1):
        to = lax.rem(y + step + 1, NY)
        copy = remote(
            y_out.at[to], y_in.at[step], send.at[len(started)], y_recv.at[step], device(x, c, to, z)
        )
        copy.start()
        started.append(copy)
        ahead.append(copy)
    for copy in ahead:
        copy.wait_recv()
    total = y_out[y]
    for step in range(NY - 1):
        total = total + y_in[step]
    z_out[...] = jnp.zeros_like(z_out)
    for step in range(NZ):
        z_out[step, 0:rows, :] = total[step * rows : (step + 1) * rows]
    ahead = []
    for step in range(NZ - 1):
        to = lax.rem(z + step + 1, NZ)
        copy = remote(
            z_out.at[to], z_in.at[step], send.at[len(started)], z_recv.at[step], device(x, c, y, to)
        )
        copy.start()
        started.append(copy)
        ahead.append(copy)
    for copy in ahead:
        copy.wait_recv()
    total = z_out[z]
    for step in range(NZ - 1):
        total = total + z_in[step]
    out[...] = total[0:rows] * factor
    for copy in started:
        copy.wait_send()


def reduce_weight(part, factor):
    height, width = part.shape
    line = height // (NX * NC)
    block = line // NY
    rows = block // NZ
    f32 = jnp.float32
    return pl.pallas_call(
        functools.partial(reduce_kernel, factor),
        out_shape=jax.ShapeDtypeStruct((rows, width), f32),
        in_specs=[pl.BlockSpec(memory_space=pltpu.VMEM)],
        out_specs=pl.BlockSpec(memory_space=pltpu.VMEM),
        scratch_shapes=[
            pltpu.VMEM((NX, line, width), f32),
            pltpu.VMEM((NX, line, width), f32),
            pltpu.VMEM((NX - 1, line, width), f32),
            pltpu.VMEM((NY, block, width), f32),
            pltpu.VMEM((NY - 1, block, width), f32),
            pltpu.VMEM((NZ, 8, width), f32),
            pltpu.VMEM((NZ - 1, 8, width), f32),
            pltpu.SemaphoreType.DMA((2 * NX + NY + NZ,)),
            pltpu.SemaphoreType.DMA((NX,)),
            pltpu.SemaphoreType.DMA((NX,)),
            pltpu.SemaphoreType.DMA((NY,)),
            pltpu.SemaphoreType.DMA((NZ,)),
        ],
        compiler_params=pltpu.CompilerParams(
            collective_id=1, has_side_effects=True, vmem_limit_bytes=50 * 1024 * 1024
        ),
    )(part)


def heads_of(matrix):
    return matrix.reshape(matrix.shape[0], matrix.shape[1] // HD, HD)


def local_allowed(keep_row, segment_len, dilation):
    count = keep_row.shape[0]
    places = jnp.arange(count, dtype=jnp.int32)
    seg_col = segment_len[:, None, None]
    rate_col = dilation[:, None, None]
    row_pos = places[None, :, None]
    col_pos = places[None, None, :]
    inside = (row_pos // seg_col == col_pos // seg_col) & (row_pos % rate_col == col_pos % rate_col)
    inside = inside & (keep_row[None, None, :] == 1)
    return inside | (row_pos == col_pos)


def scores_of(q_heads, k_heads):
    return jnp.einsum(
        "ihd,jhd->hij", q_heads, k_heads, preferred_element_type=jnp.float32
    ) * HD ** (-0.5)


def forward_part(q_heads, k_heads, v_heads, allowed):
    scores = scores_of(q_heads, k_heads)
    top_all = jnp.max(jnp.where(allowed, scores, -1e30), axis=2)
    weights = jnp.where(allowed, jnp.exp(scores - top_all[:, :, None]), 0.0)
    totals = jnp.sum(weights, axis=2)
    summed = jnp.einsum(
        "hij,jhd->ihd", weights.astype(jnp.bfloat16), v_heads, preferred_element_type=jnp.float32
    )
    return (top_all, totals, summed)


def backward_part(q_heads, k_heads, v_heads, allowed, lse, delta, d_heads):
    scale = HD ** (-0.5)
    scores = scores_of(q_heads, k_heads)
    probs = jnp.where(allowed, jnp.exp(scores - lse[:, :, None]), 0.0)
    grad_v = jnp.einsum(
        "hij,ihd->jhd", probs.astype(jnp.bfloat16), d_heads, preferred_element_type=jnp.float32
    )
    dprob = jnp.einsum("ihd,jhd->hij", d_heads, v_heads, preferred_element_type=jnp.float32)
    dscore = (probs * (dprob - delta[:, :, None])).astype(jnp.bfloat16)
    grad_q = jnp.einsum("hij,jhd->ihd", dscore, k_heads, preferred_element_type=jnp.float32) * scale
    grad_k = jnp.einsum("hij,ihd->jhd", dscore, q_heads, preferred_element_type=jnp.float32) * scale
    return (grad_q, grad_k, grad_v)


def combine(m_near, l_near, m_far, l_far):
    top_all = jnp.maximum(m_near, m_far)
    scale_near = jnp.exp(m_near - top_all)
    scale_far = jnp.exp(m_far - top_all)
    totals = scale_near * l_near + scale_far * l_far
    return (top_all, scale_near, scale_far, totals)


def local(queries, key_rows, value_rows, tissue, segment_len, dilation, out_weight, grad_out):
    q_rows = queries[0]
    k_rows = key_rows[0]
    v_rows = value_rows[0]
    keep_row = tissue[0]
    upstream = grad_out[0]
    rows, features = q_rows.shape
    groups = lax.axis_size("seq")
    per_group = rows // groups

    def to_rows(matrix):
        return matrix.reshape((per_group, groups) + matrix.shape[1:])

    def from_rows(matrix):
        return matrix.reshape((rows,) + matrix.shape[2:])

    weight_full = gather_weight(out_weight)
    d_attn = lax.dot_general(
        upstream, weight_full, (((1,), (1,)), ((), ())), preferred_element_type=jnp.float32
    ).astype(jnp.bfloat16)
    q_heads = heads_of(q_rows)
    k_heads = heads_of(k_rows)
    v_heads = heads_of(v_rows)
    d_heads = heads_of(d_attn)
    near_mask = local_allowed(keep_row, segment_len, dilation)
    m_near, l_near, acc_near = forward_part(q_heads, k_heads, v_heads, near_mask)
    g_near = jnp.sum(d_heads.astype(jnp.float32) * acc_near, axis=2).T
    moved = (
        lax.all_to_all(to_rows(q_rows), "seq", split_axis=1, concat_axis=0, tiled=True),
        lax.all_to_all(to_rows(k_rows), "seq", split_axis=1, concat_axis=0, tiled=True),
        lax.all_to_all(to_rows(v_rows), "seq", split_axis=1, concat_axis=0, tiled=True),
        lax.all_to_all(
            to_rows(keep_row.astype(jnp.bfloat16)), "seq", split_axis=1, concat_axis=0, tiled=True
        ),
        lax.all_to_all(to_rows(d_attn), "seq", split_axis=1, concat_axis=0, tiled=True),
    )
    qf_heads = heads_of(from_rows(moved[0]))
    kf_heads = heads_of(from_rows(moved[1]))
    vf_heads = heads_of(from_rows(moved[2]))
    far_mask = (from_rows(moved[3]) > 0.5)[None, None, :]
    df_heads = heads_of(from_rows(moved[4]))
    m_far, l_far, acc_far = forward_part(qf_heads, kf_heads, vf_heads, far_mask)
    g_far = jnp.sum(df_heads.astype(jnp.float32) * acc_far, axis=2).T
    back = (
        lax.all_to_all(
            acc_far.reshape(rows, 1, features), "seq", split_axis=0, concat_axis=1, tiled=True
        ),
        lax.all_to_all(m_far.T[:, None, :], "seq", split_axis=0, concat_axis=1, tiled=True),
        lax.all_to_all(l_far.T[:, None, :], "seq", split_axis=0, concat_axis=1, tiled=True),
        lax.all_to_all(g_far.T[:, None, :], "seq", split_axis=0, concat_axis=1, tiled=True),
    )
    acc_back = from_rows(back[0]).reshape(rows, features // HD, HD)
    m_back = from_rows(back[1]).T
    l_back = from_rows(back[2]).T
    g_back = from_rows(back[3]).T
    top_all, scale_near, scale_far, totals = combine(m_near, l_near, m_back, l_back)
    attn_f = (scale_near.T[:, :, None] * acc_near + scale_far.T[:, :, None] * acc_back) / totals.T[
        :, :, None
    ]
    attn = attn_f.reshape(rows, features).astype(jnp.bfloat16)
    lse = top_all + jnp.log(totals)
    delta = (scale_near * g_near + scale_far * g_back) / totals
    layer_out = jnp.dot(attn, weight_full, preferred_element_type=jnp.float32).astype(jnp.bfloat16)
    sent = (
        lax.all_to_all(to_rows(lse.T), "seq", split_axis=1, concat_axis=0, tiled=True),
        lax.all_to_all(to_rows(delta.T), "seq", split_axis=1, concat_axis=0, tiled=True),
    )
    lse_far = from_rows(sent[0]).T
    delta_far = from_rows(sent[1]).T
    gq_near, gk_near, gv_near = backward_part(
        q_heads, k_heads, v_heads, near_mask, lse, delta, d_heads
    )
    gq_far, gk_far, gv_far = backward_part(
        qf_heads, kf_heads, vf_heads, far_mask, lse_far, delta_far, df_heads
    )
    returned = (
        lax.all_to_all(
            gq_far.reshape(rows, 1, features).astype(jnp.bfloat16),
            "seq",
            split_axis=0,
            concat_axis=1,
            tiled=True,
        ),
        lax.all_to_all(
            gk_far.reshape(rows, 1, features).astype(jnp.bfloat16),
            "seq",
            split_axis=0,
            concat_axis=1,
            tiled=True,
        ),
        lax.all_to_all(
            gv_far.reshape(rows, 1, features).astype(jnp.bfloat16),
            "seq",
            split_axis=0,
            concat_axis=1,
            tiled=True,
        ),
    )
    grad_q = (gq_near.reshape(rows, features) + from_rows(returned[0]).astype(jnp.float32)).astype(
        jnp.bfloat16
    )
    grad_k = (gk_near.reshape(rows, features) + from_rows(returned[1]).astype(jnp.float32)).astype(
        jnp.bfloat16
    )
    grad_v = (gv_near.reshape(rows, features) + from_rows(returned[2]).astype(jnp.float32)).astype(
        jnp.bfloat16
    )
    share = lax.dot_general(
        attn, upstream, (((0,), (0,)), ((), ())), preferred_element_type=jnp.float32
    )
    factor = 1.0 / math.sqrt(lax.axis_size("slide") * lax.axis_size("seq") * rows)
    grad_weight = reduce_weight(share, factor)
    return (layer_out[None], grad_q[None], grad_k[None], grad_v[None], grad_weight)


def solution(mesh):
    placed = (
        P("slide", "seq", None),
        P("slide", "seq", None),
        P("slide", "seq", None),
        P("slide", "seq"),
        P(),
        P(),
        P(("slide", "seq"), None),
        P("slide", "seq", None),
    )
    return jax.shard_map(
        local,
        mesh=mesh,
        in_specs=placed,
        out_specs=(
            P("slide", "seq", None),
            P("slide", "seq", None),
            P("slide", "seq", None),
            P("slide", "seq", None),
            P(("slide", "seq"), None),
        ),
        check_vma=False,
    )
```

```python
import functools
import math

import jax
import jax.numpy as jnp
from jax import lax
from jax.experimental import pallas as pl
from jax.experimental.pallas import tpu as pltpu
from jax.sharding import PartitionSpec as P

HD = 64
PAIR = 2 * HD
NX, NC, NY, NZ = 4, 2, 4, 8
NS = NY * NZ
TILES = 256
WIDTH = 1536
EACH = TILES // NS
PAIRS = WIDTH // PAIR
CH = 2
CW = WIDTH // CH
HW = CW // 2
CP = PAIRS // CH
LINE = WIDTH // (NX * NC)
BLOCK = LINE // NY
ROWS = BLOCK // NZ
LOG2E = 1.4426950408889634
SCALE = HD**-0.5
NONE = -1e30
FLOOR = -1e29
MESH = pl.DeviceIdType.MESH
F32 = jnp.float32
BF16 = jnp.bfloat16
A_QK, A_V, A_D, A_O, A_G, A_GV = (CH * n for n in range(6))
A_F, A_L, A_S = 6 * CH, 6 * CH + 1, 6 * CH + 2
A_ALL = 6 * CH + 3


def nt(a, b):
    return lax.dot_general(a, b, (((1,), (1,)), ((), ())), preferred_element_type=F32)


def nn(a, b):
    return lax.dot_general(a, b, (((1,), (0,)), ((), ())), preferred_element_type=F32)


def tn(a, b):
    return lax.dot_general(a, b, (((0,), (0,)), ((), ())), preferred_element_type=F32)


def exact(a, b):
    return lax.dot_general(
        a, b, (((1,), (0,)), ((), ())), precision=lax.Precision.HIGHEST, preferred_element_type=F32
    )


def iota(shape, axis):
    return lax.broadcasted_iota(jnp.int32, shape, axis)


def halves():
    low = (iota((1, PAIR), 1) < HD).astype(F32)
    return low.astype(BF16), (1.0 - low).astype(BF16)


def joined(a, b):
    shape = (NS, EACH, a.shape[1])
    both = [a.astype(F32).reshape(shape), b.astype(F32).reshape(shape)]
    return jnp.concatenate(both, axis=1).astype(BF16)


def parted(block):
    wide = block.astype(F32)
    shape = (TILES, block.shape[2])
    return wide[:, :EACH].reshape(shape).astype(BF16), wide[:, EACH:].reshape(shape).astype(BF16)


def pair_at(p):
    return pl.ds(pl.multiple_of(p * PAIR, PAIR), PAIR)


def forward_pair(q, k, v, masked):
    ones = halves()
    tops, sums = [], []
    for e in range(2):
        scores = masked(e, nt(q * ones[e], k) * (SCALE * LOG2E))
        top = jnp.maximum(jnp.max(scores, axis=1, keepdims=True), FLOOR)
        weights = jnp.exp2(scores - top).astype(BF16)
        tops.append(top)
        sums.append(nn(weights, v * ones[e] + ones[1 - e]))
    low = iota((TILES, PAIR), 1) < HD
    total = pltpu.roll(jnp.where(low, sums[1], sums[0]), HD, 1)
    total = jnp.maximum(total, 1e-30)
    out = jnp.where(low, sums[0], sums[1]) / total
    lse = jnp.where(low, tops[0], tops[1]) + jnp.log(total) * LOG2E
    return out, lse


def backward_pair(q, k, v, d, masked, lse, delta):
    ones = halves()
    gq = gk = gv = None
    for e in range(2):
        qe, de, ke = q * ones[e], d * ones[e], k * ones[e]
        probs = masked(e, nt(k, qe) * (SCALE * LOG2E) - lse[e])
        dscore = (probs * (nt(v, de) - delta[e])).astype(BF16)
        terms = (tn(dscore, ke), nn(dscore, qe), nn(probs.astype(BF16), de))
        gq, gk, gv = terms if e == 0 else (gq + terms[0], gk + terms[1], gv + terms[2])
    return gq * SCALE, gk * SCALE, gv


def remote(src, dst, send, recv, peer):
    return pltpu.make_async_remote_copy(
        src_ref=src, dst_ref=dst, send_sem=send, recv_sem=recv, device_id=peer, device_id_type=MESH
    )


def kernel(
    factor,
    q_in, k_in, v_in, g_in, keep_in, seg, dil, w_in,
    out_lo, out_q, out_k, out_v, out_w,
    qp, kp, vp, gp, dp, qf, kf, vf, df, of, o_near, attn, attn_t, nq, nk, nv,
    x_fwd, x_bwd, stat, stat_t, far_t, bias_row, bias_col,
    qk_s, v_s, d_s, qk_r, v_r, d_r, o_r, g_r, gv_r,
    f_s, f_r, l_s, l_r, s_s, s_r,
    w_src, w_z, w_full,
    c_s, c_r, own, x_s, x_r, y_s, y_r, z_s, z_r,
    a_send, a_recv, w_send, wz_recv, wy_recv, wx_recv, wc_recv,
    r_send, rc_recv, rx_recv, ry_recv, rz_recv,
):
    slide = lax.axis_index("slide")
    me = lax.axis_index("seq")
    x, c = lax.div(slide, NC), lax.rem(slide, NC)
    y, z = lax.div(me, NZ), lax.rem(me, NZ)

    def device(xx, cc, yy, zz):
        return (xx * NC + cc, yy * NZ + zz)

    def peer_of(n):
        return lax.rem(y + lax.div(n, NZ), NY) * NZ + lax.rem(z + lax.rem(n, NZ), NZ)

    sibling = device(x, 1 - c, y, z)
    barrier = pltpu.get_barrier_semaphore()

    def greet(n, carry):
        pl.semaphore_signal(barrier, inc=1, device_id=(slide, peer_of(n)), device_id_type=MESH)
        return carry

    lax.fori_loop(1, NS, greet, 0)
    for peer in [sibling] + [device(lax.rem(x + step, NX), c, y, z) for step in range(1, NX)]:
        pl.semaphore_signal(barrier, inc=1, device_id=peer, device_id_type=MESH)
    pl.semaphore_wait(barrier, NS - 1 + NX)

    def exchange(src, dst, k):
        def body(n, carry):
            peer = peer_of(n)
            remote(src.at[peer], dst.at[me], a_send.at[k], a_recv.at[k], (slide, peer)).start()
            return carry

        lax.fori_loop(1, NS, body, 0)
        dst.at[me][...] = src.at[me][...]

    def arrived(dst, k):
        part = dst.at[pl.ds(0, NS - 1)]
        pltpu.make_async_copy(part, part, a_recv.at[k]).wait()

    def departed(src, k):
        part = src.at[pl.ds(0, NS - 1)]
        pltpu.make_async_copy(part, part, a_send.at[k]).wait()

    w_started, r_started = [], []

    def send_w(src, dst, recv, peer):
        copy = remote(src, dst, w_send.at[len(w_started)], recv, peer)
        copy.start()
        w_started.append(copy)
        return copy

    def send_r(src, dst, recv, peer):
        copy = remote(src, dst, r_send.at[len(r_started)], recv, peer)
        copy.start()
        r_started.append(copy)
        return copy

    def line_of(xx, cc):
        return pl.ds(pl.multiple_of((xx * NC + cc) * LINE, 16), LINE)

    w_src[...] = jnp.zeros_like(w_src)
    w_src[0:ROWS, :] = w_in[...]
    w_z[z] = w_src[...]
    wz = [
        send_w(w_src, w_z.at[z], wz_recv.at[step - 1], device(x, c, y, lax.rem(z + step, NZ)))
        for step in range(1, NZ)
    ]

    square = (TILES, TILES)
    line, lane = iota(square, 0), iota(square, 1)
    order = (lane == lax.rem(line, EACH) * NS + lax.div(line, EACH)).astype(F32).astype(BF16)
    back = (lane == lax.rem(line, NS) * EACH + lax.div(line, NS)).astype(F32).astype(BF16)
    for ch in range(CH):
        cols = pl.ds(ch * CW, CW)
        q = nn(order, q_in[:, cols])
        k = nn(order, k_in[:, cols])
        qk_s[ch] = joined(q, k)
        exchange(qk_s.at[ch], qk_r.at[ch], A_QK + ch)
        qp[:, cols] = q.astype(BF16)
        kp[:, cols] = k.astype(BF16)
        v = nn(order, v_in[:, cols])
        v_s[ch] = joined(v[:, :HW], v[:, HW:])
        exchange(v_s.at[ch], v_r.at[ch], A_V + ch)
        vp[:, cols] = v.astype(BF16)
        if ch == 0:
            keep = keep_in[...].astype(F32).astype(BF16)
            keep_cols = nt(order, jnp.broadcast_to(keep, (PAIR, TILES)))
            f_s[...] = keep_cols.reshape(NS, EACH, PAIR)
            exchange(f_s, f_r, A_F)
    for ch in range(CH):
        cols = pl.ds(ch * CW, CW)
        gp[:, cols] = nn(order, g_in[:, cols]).astype(BF16)

    keep_row = nt(jnp.broadcast_to(keep, (16, TILES)), order)[0:1]
    pos_l = lax.rem(line, EACH) * NS + lax.div(line, EACH)
    pos_c = lax.rem(lane, EACH) * NS + lax.div(lane, EACH)
    apart = lax.bitwise_xor(pos_l, pos_c)
    same = line == lane
    x_fwd[...] = jnp.where(same, 0, apart + jnp.where(keep_row > 0.5, 0, 65536))
    keep_wide = jnp.concatenate([keep_cols, keep_cols], axis=1)
    x_bwd[...] = jnp.where(same, 0, apart + jnp.where(keep_wide > 0.5, 0, 65536))

    def bits(p, e):
        head = 2 * p + e
        return 65536 + (TILES - seg[head]) + (dil[head] - 1)

    for copy in wz:
        copy.wait_recv()
    out_row = iota((BLOCK, NZ * 16), 0)
    in_row = iota((BLOCK, NZ * 16), 1)
    pick = (in_row == lax.div(out_row, ROWS) * 16 + lax.rem(out_row, ROWS)).astype(F32).astype(BF16)
    mine = pl.ds(pl.multiple_of(((x * NC + c) * NY + y) * BLOCK, 16), BLOCK)
    w_full[mine, :] = nn(pick, w_z[...].reshape(NZ * 16, WIDTH)).astype(BF16)
    wy = [
        send_w(w_full.at[mine], w_full.at[mine], wy_recv.at[step - 1], device(x, c, lax.rem(y + step, NY), z))
        for step in range(1, NY)
    ]

    def put_stat(p, stats, values):
        return jnp.where(lax.rem(iota((TILES, PAIR), 1), HD) == p, values, stats)

    def near_forward(p, stats):
        at = pair_at(p)

        def masked(e, scores):
            return jnp.where(lax.bitwise_and(x_fwd[...], bits(p, e)) == 0, scores, NONE)

        out, lse = forward_pair(qp[:, at], kp[:, at], vp[:, at], masked)
        o_near[:, at] = out
        return put_stat(p, stats, lse)

    near_lse = lax.fori_loop(0, 3, near_forward, jnp.zeros((TILES, PAIR), F32))

    for copy in wy:
        copy.wait_recv()
    mine = line_of(x, c)
    wx = [
        send_w(w_full.at[mine], w_full.at[mine], wx_recv.at[step - 1], device(lax.rem(x + step, NX), c, y, z))
        for step in range(1, NX)
    ]
    wc = [send_w(w_full.at[mine], w_full.at[mine], wc_recv.at[0], sibling)]
    near_lse = lax.fori_loop(3, PAIRS, near_forward, near_lse)
    stat[...] = near_lse

    arrived(f_r, A_F)
    flags = f_r[...].reshape(TILES, PAIR)
    bias = jnp.where(flags > 0.5, 0.0, NONE)
    bias_col[...] = jnp.concatenate([bias, bias], axis=1)
    bias_row[...] = jnp.transpose(bias)[0:8]

    def far_forward(p, stats):
        at = pair_at(p)
        out, lse = forward_pair(
            qf[:, at], kf[:, at], vf[:, at], lambda e, scores: scores + bias_row[0:1, :]
        )
        of[:, at] = out.astype(BF16)
        return put_stat(p, stats, lse)

    far_lse = jnp.zeros((TILES, PAIR), F32)
    for ch in range(CH):
        cols, low, high = pl.ds(ch * CW, CW), pl.ds(ch * CW, HW), pl.ds(ch * CW + HW, HW)
        arrived(qk_r.at[ch], A_QK + ch)
        qf[:, cols], kf[:, cols] = parted(qk_r[ch])
        arrived(v_r.at[ch], A_V + ch)
        vf[:, low], vf[:, high] = parted(v_r[ch])
        far_lse = lax.fori_loop(ch * CP, (ch + 1) * CP, far_forward, far_lse)
        departed(v_s.at[ch], A_V + ch)
        v_s[ch] = joined(of[:, low], of[:, high])
        exchange(v_s.at[ch], o_r.at[ch], A_O + ch)
    l_s[...] = far_lse.reshape(NS, EACH, PAIR)
    exchange(l_s, l_r, A_L)

    for step in range(1, NX):
        wx[step - 1].wait_recv()
        there = line_of(lax.rem(x + NX - step, NX), c)
        wc.append(send_w(w_full.at[there], w_full.at[there], wc_recv.at[step], sibling))
    for copy in wc:
        copy.wait_recv()
    for ch in range(CH):
        for half in range(2):
            cols = pl.ds(ch * CW + half * HW, HW)
            dp[:, cols] = nt(gp[...], w_full[cols, :]).astype(BF16)
        low, high = pl.ds(ch * CW, HW), pl.ds(ch * CW + HW, HW)
        d_s[ch] = joined(dp[:, low], dp[:, high])
        exchange(d_s.at[ch], d_r.at[ch], A_D + ch)

    arrived(l_r, A_L)
    lse_near = stat[...]
    lse_far = l_r[...].reshape(TILES, PAIR)
    top = jnp.maximum(lse_near, lse_far)
    lse = top + jnp.log(jnp.exp2(lse_near - top) + jnp.exp2(lse_far - top)) * LOG2E
    share_near = jnp.exp2(lse_near - lse)
    share_far = jnp.exp2(lse_far - lse)
    for ch in range(CH):
        low, high = pl.ds(ch * CW, HW), pl.ds(ch * CW + HW, HW)
        arrived(o_r.at[ch], A_O + ch)
        of[:, low], of[:, high] = parted(o_r[ch])

    def combine(p, delta):
        at = pair_at(p)
        small = (PAIR, PAIR)
        first, second = iota(small, 0), iota(small, 1)
        together = (first < HD) == (second < HD)
        spread = (together & (lax.rem(first, HD) == p)).astype(F32)
        gather = (together & (lax.rem(second, HD) == p + 16)).astype(F32)
        whole = exact(share_near, spread) * o_near[:, at] + exact(share_far, spread) * of[:, at].astype(F32)
        attn[:, at] = whole.astype(BF16)
        attn_t[at, :] = jnp.transpose(whole).astype(BF16)
        return delta + exact(whole * dp[:, at].astype(F32), gather)

    delta = lax.fori_loop(0, PAIRS, combine, jnp.zeros((TILES, PAIR), F32))
    stats = jnp.where(lax.rem(iota((TILES, PAIR), 1), HD) < 16, lse, delta)
    s_s[...] = stats.reshape(NS, EACH, PAIR)
    exchange(s_s, s_r, A_S)
    stat_t[...] = jnp.transpose(stats)

    for step in range(NX):
        to = lax.rem(x + step + 1, NX)
        c_s[step] = nn(attn_t[line_of(to, 1 - c), :], gp[...]).astype(BF16)
        send_r(c_s.at[step], c_r.at[step], rc_recv.at[step], sibling)

    def rows_of(table, p):
        lse = [table[pl.ds(p + HD * e, 1), :] for e in range(2)]
        delta = [table[pl.ds(p + HD * e + 16, 1), :] for e in range(2)]
        return lse, delta

    arrived(s_r, A_S)
    far_t[...] = jnp.transpose(s_r[...].reshape(TILES, PAIR))

    def far_backward(ch, p, carry):
        at = pair_at(p)
        here = pair_at(p - ch * CP)
        gq, gk, gv = backward_pair(
            qf[:, at], kf[:, at], vf[:, at], df[:, at],
            lambda e, scores: jnp.exp2(scores + bias_col[...]), *rows_of(far_t, p),
        )
        qk_s[ch, :, :, here] = joined(gq, gk)
        of[:, at] = gv.astype(BF16)
        return carry

    for ch in range(CH):
        low, high = pl.ds(ch * CW, HW), pl.ds(ch * CW + HW, HW)
        arrived(d_r.at[ch], A_D + ch)
        df[:, low], df[:, high] = parted(d_r[ch])
        departed(qk_s.at[ch], A_QK + ch)
        lax.fori_loop(ch * CP, (ch + 1) * CP, functools.partial(far_backward, ch), 0)
        exchange(qk_s.at[ch], g_r.at[ch], A_G + ch)
        departed(d_s.at[ch], A_D + ch)
        d_s[ch] = joined(of[:, low], of[:, high])
        exchange(d_s.at[ch], gv_r.at[ch], A_GV + ch)

    ahead = []
    for step in range(NX):
        to = lax.rem(x + step + 1, NX)
        r_started[step].wait_recv()
        total = nn(attn_t[line_of(to, c), :], gp[...]) + c_r[step].astype(F32)
        if step < NX - 1:
            x_s[step] = total.astype(BF16)
            ahead.append(send_r(x_s.at[step], x_r.at[step], rx_recv.at[step], device(to, c, y, z)))
        else:
            own[...] = total

    def near_backward(p, carry):
        at = pair_at(p)

        def masked(e, scores):
            return jnp.where(lax.bitwise_and(x_bwd[...], bits(p, e)) == 0, jnp.exp2(scores), 0.0)

        nq[:, at], nk[:, at], nv[:, at] = backward_pair(
            qp[:, at], kp[:, at], vp[:, at], dp[:, at], masked, *rows_of(stat_t, p)
        )
        return carry

    lax.fori_loop(0, PAIRS // 2, near_backward, 0)
    for copy in ahead:
        copy.wait_recv()
    total = own[...]
    for step in range(NX - 1):
        total = total + x_r[step].astype(F32)
    y_s[...] = total.reshape(NY, BLOCK, WIDTH)
    ahead = []
    for step in range(NY - 1):
        to = lax.rem(y + step + 1, NY)
        ahead.append(send_r(y_s.at[to], y_r.at[step], ry_recv.at[step], device(x, c, to, z)))
    lax.fori_loop(PAIRS // 2, PAIRS, near_backward, 0)
    for copy in ahead:
        copy.wait_recv()
    total = y_s[y]
    for step in range(NY - 1):
        total = total + y_r[step]
    z_s[...] = jnp.zeros_like(z_s)
    for step in range(NZ):
        z_s[step, 0:ROWS, :] = total[step * ROWS : (step + 1) * ROWS]
    ahead = []
    for step in range(NZ - 1):
        to = lax.rem(z + step + 1, NZ)
        ahead.append(send_r(z_s.at[to], z_r.at[step], rz_recv.at[step], device(x, c, y, to)))

    for ch in range(CH):
        cols = pl.ds(ch * CW, CW)
        done = nn(attn[...], w_full[:, cols]).astype(BF16)
        out_lo[:, cols] = nn(back, done).astype(BF16)

    for ch in range(CH):
        cols, low, high = pl.ds(ch * CW, CW), pl.ds(ch * CW, HW), pl.ds(ch * CW + HW, HW)
        arrived(g_r.at[ch], A_G + ch)
        far_q, far_k = parted(g_r[ch])
        out_q[:, cols] = nn(back, (nq[:, cols] + far_q.astype(F32)).astype(BF16)).astype(BF16)
        out_k[:, cols] = nn(back, (nk[:, cols] + far_k.astype(F32)).astype(BF16)).astype(BF16)
        arrived(gv_r.at[ch], A_GV + ch)
        far_low, far_high = parted(gv_r[ch])
        out_v[:, low] = nn(back, (nv[:, low] + far_low.astype(F32)).astype(BF16)).astype(BF16)
        out_v[:, high] = nn(back, (nv[:, high] + far_high.astype(F32)).astype(BF16)).astype(BF16)

    for copy in ahead:
        copy.wait_recv()
    total = z_s[z]
    for step in range(NZ - 1):
        total = total + z_r[step]
    out_w[...] = total[0:ROWS] * factor
    for copy in w_started + r_started:
        copy.wait_send()
    for ch in range(CH):
        departed(v_s.at[ch], A_O + ch)
        departed(qk_s.at[ch], A_G + ch)
        departed(d_s.at[ch], A_GV + ch)
    departed(f_s, A_F)
    departed(l_s, A_L)
    departed(s_s, A_S)


def layer(queries, key_rows, value_rows, tissue, segment_len, dilation, out_weight, grad_out):
    shape = (TILES, WIDTH)
    vmem = pl.BlockSpec(memory_space=pltpu.VMEM)
    smem = pl.BlockSpec(memory_space=pltpu.SMEM)
    low, wide = pltpu.VMEM(shape, BF16), pltpu.VMEM(shape, F32)
    stats = pltpu.VMEM((NS, EACH, PAIR), F32)
    table = pltpu.VMEM((PAIR, TILES), F32)
    square = pltpu.VMEM((TILES, TILES), jnp.int32)
    both = pltpu.VMEM((CH, NS, 2 * EACH, CW), BF16)
    single = pltpu.VMEM((CH, NS, 2 * EACH, HW), BF16)
    dma = pltpu.SemaphoreType.DMA
    factor = 1.0 / math.sqrt(NX * NC * NS * TILES)
    outs = pl.pallas_call(
        functools.partial(kernel, factor),
        out_shape=[jax.ShapeDtypeStruct(shape, BF16)] * 4 + [jax.ShapeDtypeStruct((ROWS, WIDTH), F32)],
        in_specs=[vmem] * 5 + [smem] * 2 + [vmem],
        out_specs=[vmem] * 5,
        scratch_shapes=[low] * 10 + [wide] + [low, pltpu.VMEM((WIDTH, TILES), BF16)] + [wide] * 3
        + [square] * 2 + [pltpu.VMEM((TILES, PAIR), F32), table, table]
        + [pltpu.VMEM((8, TILES), F32), pltpu.VMEM((TILES, TILES), F32)]
        + [both, single, single, both, single, single, single, both, single]
        + [stats] * 6
        + [
            pltpu.VMEM((16, WIDTH), BF16),
            pltpu.VMEM((NZ, 16, WIDTH), BF16),
            pltpu.VMEM((WIDTH, WIDTH), BF16),
            pltpu.VMEM((NX, LINE, WIDTH), BF16),
            pltpu.VMEM((NX, LINE, WIDTH), BF16),
            pltpu.VMEM((LINE, WIDTH), F32),
            pltpu.VMEM((NX - 1, LINE, WIDTH), BF16),
            pltpu.VMEM((NX - 1, LINE, WIDTH), BF16),
            pltpu.VMEM((NY, BLOCK, WIDTH), F32),
            pltpu.VMEM((NY - 1, BLOCK, WIDTH), F32),
            pltpu.VMEM((NZ, 8, WIDTH), F32),
            pltpu.VMEM((NZ - 1, 8, WIDTH), F32),
            dma((A_ALL,)),
            dma((A_ALL,)),
            dma((NZ + NY + 2 * NX,)),
            dma((NZ,)),
            dma((NY,)),
            dma((NX,)),
            dma((NX,)),
            dma((NZ + NY + 2 * NX,)),
            dma((NX,)),
            dma((NX,)),
            dma((NY,)),
            dma((NZ,)),
        ],
        compiler_params=pltpu.CompilerParams(
            collective_id=0, has_side_effects=True, vmem_limit_bytes=60 * 1024 * 1024
        ),
    )(
        queries[0], key_rows[0], value_rows[0], grad_out[0], tissue, segment_len, dilation, out_weight
    )
    return tuple(out[None] for out in outs[:4]) + (outs[4],)


def solution(mesh):
    tiles = P("slide", "seq", None)
    rows = P(("slide", "seq"), None)
    return jax.shard_map(
        layer,
        mesh=mesh,
        in_specs=(tiles, tiles, tiles, P("slide", "seq"), P(), P(), rows, tiles),
        out_specs=(tiles, tiles, tiles, tiles, rows),
        check_vma=False,
    )
```

```python
import functools
import math

import jax
import jax.numpy as jnp
from jax import lax
from jax.experimental import pallas as pl
from jax.experimental.pallas import tpu as pltpu
from jax.sharding import PartitionSpec as P

HD = 64
PAIR = 2 * HD
NX, NC, NY, NZ = 4, 2, 4, 8
NS = NY * NZ
TILES = 256
WIDTH = 1536
EACH = TILES // NS
PAIRS = WIDTH // PAIR
CH = 3
CW = WIDTH // CH
HW = CW // 2
CP = PAIRS // CH
LINE = WIDTH // (NX * NC)
BLOCK = LINE // NY
ROWS = BLOCK // NZ
CHUNKS = WIDTH // PAIR
PACK = 80
FLAG = 100.0
LOG2E = 1.4426950408889634
SCALE = HD**-0.5
NONE = -1e30
FLOOR = -1e29
MESH = pl.DeviceIdType.MESH
F32 = jnp.float32
BF16 = jnp.bfloat16
A_QK, A_V, A_O, A_G, A_GV, A_L, A_S = (CH * n for n in range(7))
A_GO = 7 * CH
A_ALL = 7 * CH + 1
SLOTS = PAIR // EACH


def nt(a, b):
    return lax.dot_general(a, b, (((1,), (1,)), ((), ())), preferred_element_type=F32)


def nn(a, b):
    return lax.dot_general(a, b, (((1,), (0,)), ((), ())), preferred_element_type=F32)


def tn(a, b):
    return lax.dot_general(a, b, (((0,), (0,)), ((), ())), preferred_element_type=F32)


def doubled(value):
    high = value.astype(BF16)
    return jnp.concatenate([high, (value - high.astype(F32)).astype(BF16)], axis=1)


def tripled(value):
    high = value.astype(BF16)
    rest = value - high.astype(F32)
    middle = rest.astype(BF16)
    return jnp.concatenate([high, middle, (rest - middle.astype(F32)).astype(BF16)], axis=1)


def slot_lane(lane):
    slot = lax.rem(lane, SLOTS)
    inner = lax.rem(slot, SLOTS // 2)
    return lax.div(inner, 2) + HD * lax.rem(inner, 2) + 16 * lax.div(slot, SLOTS // 2)


def own_slots():
    shape = (TILES, PAIR)
    return lax.div(iota(shape, 1), SLOTS) == lax.rem(iota(shape, 0), EACH)


def folded(stats):
    tall = (3 * PAIR, PAIR)
    move = (lax.rem(iota(tall, 0), PAIR) == slot_lane(iota(tall, 1))).astype(F32).astype(BF16)
    spread = jnp.where(own_slots(), nn(tripled(stats), move), 0.0)
    return jnp.sum(spread.reshape(NS, EACH, PAIR), axis=1, keepdims=True)


def unfolded(rows):
    tall = (3 * PAIR, PAIR)
    move = (slot_lane(lax.rem(iota(tall, 0), PAIR)) == iota(tall, 1)).astype(F32).astype(BF16)
    spread = jnp.broadcast_to(rows, (NS, EACH, PAIR)).reshape(TILES, PAIR)
    return nn(tripled(jnp.where(own_slots(), spread, 0.0)), move)


def iota(shape, axis):
    return lax.broadcasted_iota(jnp.int32, shape, axis)


def halves():
    low = (iota((1, PAIR), 1) < HD).astype(F32)
    return low.astype(BF16), (1.0 - low).astype(BF16)


def joined(a, b):
    shape = (NS, EACH, a.shape[1])
    both = [a.astype(F32).reshape(shape), b.astype(F32).reshape(shape)]
    return jnp.concatenate(both, axis=1).astype(BF16)


def parted(block):
    wide = block.astype(F32)
    shape = (TILES, block.shape[2])
    return wide[:, :EACH].reshape(shape).astype(BF16), wide[:, EACH:].reshape(shape).astype(BF16)


def unfold():
    line = iota((CHUNKS * BLOCK, PAIR), 0)
    inner = lax.rem(line, BLOCK)
    want = lax.div(inner, ROWS) * PACK + lax.div(line, BLOCK) * ROWS + lax.rem(inner, ROWS)
    lane = iota((CHUNKS * BLOCK, PAIR), 1)
    parts = [(lane + PAIR * n == want).astype(F32).astype(BF16) for n in range(NZ * PACK // PAIR)]
    return jnp.concatenate(parts, axis=1)


def stacked(value):
    return jnp.concatenate([value[:, n * PAIR : (n + 1) * PAIR] for n in range(CHUNKS)], axis=0)


def pair_at(p):
    return pl.ds(pl.multiple_of(p * PAIR, PAIR), PAIR)


def forward_pair(q, k, v, masked):
    ones = halves()
    tops, sums = [], []
    for e in range(2):
        scores = masked(e, nt(q * ones[e], k) * (SCALE * LOG2E))
        top = jnp.maximum(jnp.max(scores, axis=1, keepdims=True), FLOOR)
        weights = jnp.exp2(scores - top).astype(BF16)
        tops.append(top)
        sums.append(nn(weights, v * ones[e] + ones[1 - e]))
    low = iota((TILES, PAIR), 1) < HD
    total = pltpu.roll(jnp.where(low, sums[1], sums[0]), HD, 1)
    total = jnp.maximum(total, 1e-30)
    out = jnp.where(low, sums[0], sums[1]) / total
    lse = jnp.where(low, tops[0], tops[1]) + jnp.log(total) * LOG2E
    return out, lse


def backward_pair(q, k, v, d, masked, lse, delta):
    ones = halves()
    gq = gk = gv = None
    for e in range(2):
        qe, de, ke = q * ones[e], d * ones[e], k * ones[e]
        probs = masked(e, nt(k, qe) * (SCALE * LOG2E) - lse[e])
        dscore = (probs * (nt(v, de) - delta[e])).astype(BF16)
        terms = (tn(dscore, ke), nn(dscore, qe), nn(probs.astype(BF16), de))
        gq, gk, gv = terms if e == 0 else (gq + terms[0], gk + terms[1], gv + terms[2])
    return gq * SCALE, gk * SCALE, gv


def remote(src, dst, send, recv, peer):
    return pltpu.make_async_remote_copy(
        src_ref=src, dst_ref=dst, send_sem=send, recv_sem=recv, device_id=peer, device_id_type=MESH
    )


def kernel(
    factor,
    q_in, k_in, v_in, g_in, keep_in, seg, dil, w_in,
    out_lo, out_q, out_k, out_v, out_w,
    qp, kp, vp, gp, dp, qf, kf, vf, gf, df, of, o_near, attn, attn_t, nq, nk, nv,
    x_fwd, x_bwd, stat, stat_t, far_t, bias_row, bias_col,
    qk_s, v_s, gv_s, qk_r, v_r, o_r, g_r, gv_r, go_s, go_r,
    l_s, l_r, s_s, s_r,
    w_pad, w_src, w_z, w_full,
    c_s, c_r, own, x_s, x_r, y_s, y_r, z_s, z_r,
    a_send, a_recv, w_send, wz_recv, wy_recv, wx_recv, wc_recv,
    r_send, rc_recv, rx_recv, ry_recv, rz_recv,
):
    slide = lax.axis_index("slide")
    me = lax.axis_index("seq")
    x, c = lax.div(slide, NC), lax.rem(slide, NC)
    y, z = lax.div(me, NZ), lax.rem(me, NZ)

    def device(xx, cc, yy, zz):
        return (xx * NC + cc, yy * NZ + zz)

    def peer_of(n):
        return lax.rem(y + lax.div(n, NZ), NY) * NZ + lax.rem(z + lax.rem(n, NZ), NZ)

    sibling = device(x, 1 - c, y, z)
    barrier = pltpu.get_barrier_semaphore()

    def greet(n, carry):
        pl.semaphore_signal(barrier, inc=1, device_id=(slide, peer_of(n)), device_id_type=MESH)
        return carry

    lax.fori_loop(1, NS, greet, 0)
    for peer in [sibling] + [device(lax.rem(x + step, NX), c, y, z) for step in range(1, NX)]:
        pl.semaphore_signal(barrier, inc=1, device_id=peer, device_id_type=MESH)

    def exchange(src, dst, k):
        def body(n, carry):
            peer = peer_of(n)
            remote(src.at[peer], dst.at[me], a_send.at[k], a_recv.at[k], (slide, peer)).start()
            return carry

        lax.fori_loop(1, NS, body, 0)
        dst.at[me][...] = src.at[me][...]

    def arrived(dst, k):
        part = dst.at[pl.ds(0, NS - 1)]
        pltpu.make_async_copy(part, part, a_recv.at[k]).wait()

    def departed(src, k):
        part = src.at[pl.ds(0, NS - 1)]
        pltpu.make_async_copy(part, part, a_send.at[k]).wait()

    w_started, r_started = [], []

    def send_w(src, dst, recv, peer):
        copy = remote(src, dst, w_send.at[len(w_started)], recv, peer)
        copy.start()
        w_started.append(copy)
        return copy

    def send_r(src, dst, recv, peer):
        copy = remote(src, dst, r_send.at[len(r_started)], recv, peer)
        copy.start()
        r_started.append(copy)
        return copy

    def line_of(xx, cc):
        return pl.ds(pl.multiple_of((xx * NC + cc) * LINE, 16), LINE)

    w_pad[...] = jnp.zeros_like(w_pad)
    w_pad[0:ROWS, :] = w_in[...]
    out_row, in_row = iota((PACK, CHUNKS * 16), 0), iota((PACK, CHUNKS * 16), 1)
    chosen = (lax.div(out_row, ROWS) == lax.div(in_row, 16)) & (lax.rem(out_row, ROWS) == lax.rem(in_row, 16))
    w_src[...] = nn(chosen.astype(F32).astype(BF16), stacked(w_pad[...])).astype(BF16)
    w_z[z] = w_src[...]
    pl.semaphore_wait(barrier, NS - 1 + NX)
    wz = [
        send_w(w_src, w_z.at[z], wz_recv.at[step - 1], device(x, c, y, lax.rem(z + step, NZ)))
        for step in range(1, NZ)
    ]

    square = (TILES, TILES)
    line, lane = iota(square, 0), iota(square, 1)
    order = (lane == lax.rem(line, EACH) * NS + lax.div(line, EACH)).astype(F32).astype(BF16)
    back = (lane == lax.rem(line, NS) * EACH + lax.div(line, NS)).astype(F32).astype(BF16)
    keep = keep_in[...].astype(F32).astype(BF16)
    keep_cols = nt(order, jnp.broadcast_to(keep, (PAIR, TILES)))
    keep_wide = jnp.concatenate([keep_cols] * (CW // PAIR), axis=1) > 0.5
    for ch in range(CH):
        cols = pl.ds(ch * CW, CW)
        q = nn(order, q_in[:, cols])
        k = nn(order, k_in[:, cols])
        qk_s[ch] = joined(q, jnp.where(keep_wide, k, FLAG))
        exchange(qk_s.at[ch], qk_r.at[ch], A_QK + ch)
        qp[:, cols] = q.astype(BF16)
        kp[:, cols] = k.astype(BF16)
        v = nn(order, v_in[:, cols])
        v_s[ch] = joined(v[:, :HW], v[:, HW:])
        exchange(v_s.at[ch], v_r.at[ch], A_V + ch)
        vp[:, cols] = v.astype(BF16)
        if ch == 0:
            half = WIDTH // 2
            ends = []
            for cols in (pl.ds(0, half), pl.ds(half, half)):
                ends.append(nn(order, g_in[:, cols]))
                gp[:, cols] = ends[-1].astype(BF16)
            go_s[...] = joined(*ends)
            exchange(go_s, go_r, A_GO)

    keep_row = nt(jnp.broadcast_to(keep, (16, TILES)), order)[0:1]
    pos_l = lax.rem(line, EACH) * NS + lax.div(line, EACH)
    pos_c = lax.rem(lane, EACH) * NS + lax.div(lane, EACH)
    apart = lax.bitwise_xor(pos_l, pos_c)
    same = line == lane
    x_fwd[...] = jnp.where(same, 0, apart + jnp.where(keep_row > 0.5, 0, 65536))
    x_bwd[...] = jnp.where(same, 0, apart + jnp.where(keep_wide[:, :TILES], 0, 65536))

    def bits(p, e):
        head = 2 * p + e
        return 65536 + (TILES - seg[head]) + (dil[head] - 1)

    for copy in wz:
        copy.wait_recv()
    mine = pl.ds(pl.multiple_of(((x * NC + c) * NY + y) * BLOCK, 16), BLOCK)
    rows = nn(unfold(), w_z[...].reshape(NZ * PACK, PAIR)).astype(BF16)
    for n in range(CHUNKS):
        w_full[mine, n * PAIR : (n + 1) * PAIR] = rows[n * BLOCK : (n + 1) * BLOCK]
    wy = [
        send_w(w_full.at[mine], w_full.at[mine], wy_recv.at[step - 1], device(x, c, lax.rem(y + step, NY), z))
        for step in range(1, NY)
    ]

    def put_stat(p, stats, values):
        return jnp.where(lax.rem(iota((TILES, PAIR), 1), HD) == p, values, stats)

    def near_forward(ch, p, stats):
        at = pair_at(p)

        def masked(e, scores):
            return jnp.where(lax.bitwise_and(x_fwd[...], bits(p, e)) == 0, scores, NONE)

        out, lse = forward_pair(qp[:, at], kp[:, at], vp[:, at], masked)
        o_near[:, at] = out
        return put_stat(p - ch * CP, stats, lse)

    def near_chunk(ch):
        empty = jnp.zeros((TILES, PAIR), F32)
        stat[ch] = lax.fori_loop(ch * CP, (ch + 1) * CP, functools.partial(near_forward, ch), empty)

    near_chunk(0)

    for copy in wy:
        copy.wait_recv()
    mine = line_of(x, c)
    wx = [
        send_w(w_full.at[mine], w_full.at[mine], wx_recv.at[step - 1], device(lax.rem(x + step, NX), c, y, z))
        for step in range(1, NX)
    ]
    wc = [send_w(w_full.at[mine], w_full.at[mine], wc_recv.at[0], sibling)]
    for ch in range(1, CH):
        near_chunk(ch)

    def columns(ch):
        return pl.ds(ch * CW, CW), pl.ds(ch * CW, HW), pl.ds(ch * CW + HW, HW)

    def far_forward(ch, p, stats):
        at = pair_at(p)
        out, lse = forward_pair(
            qf[:, at], kf[:, at], vf[:, at], lambda e, scores: scores + bias_row[0:1, :]
        )
        of[:, at] = out.astype(BF16)
        return put_stat(p - ch * CP, stats, lse)

    def far_chunk(ch):
        cols, low, high = columns(ch)
        arrived(qk_r.at[ch], A_QK + ch)
        qf[:, cols], kf[:, cols] = parted(qk_r[ch])
        if ch == 0:
            bias = jnp.where(kf[:, 0:PAIR].astype(F32) > FLAG / 2, NONE, 0.0)
            bias_col[...] = jnp.concatenate([bias, bias], axis=1)
            bias_row[...] = jnp.transpose(bias)[0:8]
        arrived(v_r.at[ch], A_V + ch)
        vf[:, low], vf[:, high] = parted(v_r[ch])
        empty = jnp.zeros((TILES, PAIR), F32)
        lse = lax.fori_loop(ch * CP, (ch + 1) * CP, functools.partial(far_forward, ch), empty)
        departed(v_s.at[ch], A_V + ch)
        v_s[ch] = joined(of[:, low], of[:, high])
        exchange(v_s.at[ch], o_r.at[ch], A_O + ch)
        l_s[ch] = folded(lse)
        exchange(l_s.at[ch], l_r.at[ch], A_L + ch)

    def combine(ch, share_near, share_far, p, delta):
        at = pair_at(p)
        near = p - ch * CP
        tall = (2 * PAIR, PAIR)
        first, second = lax.rem(iota(tall, 0), PAIR), iota(tall, 1)
        together = (first < HD) == (second < HD)
        spread = (together & (lax.rem(first, HD) == near)).astype(F32).astype(BF16)
        gather = (together & (lax.rem(second, HD) == near + 16)).astype(F32).astype(BF16)
        far = of[:, at].astype(F32)
        whole = nn(share_near, spread) * o_near[:, at] + nn(share_far, spread) * far
        attn[:, at] = whole.astype(BF16)
        attn_t[at, :] = jnp.transpose(whole).astype(BF16)
        return delta + nn(doubled(whole * dp[:, at].astype(F32)), gather)

    def combine_chunk(ch):
        cols, low, high = columns(ch)
        arrived(l_r.at[ch], A_L + ch)
        lse_near = stat[ch]
        lse_far = unfolded(l_r[ch])
        top = jnp.maximum(lse_near, lse_far)
        lse = top + jnp.log(jnp.exp2(lse_near - top) + jnp.exp2(lse_far - top)) * LOG2E
        share_near = doubled(jnp.exp2(lse_near - lse))
        share_far = doubled(jnp.exp2(lse_far - lse))
        arrived(o_r.at[ch], A_O + ch)
        of[:, low], of[:, high] = parted(o_r[ch])
        body = functools.partial(combine, ch, share_near, share_far)
        delta = lax.fori_loop(ch * CP, (ch + 1) * CP, body, jnp.zeros((TILES, PAIR), F32))
        stats = jnp.where(lax.rem(iota((TILES, PAIR), 1), HD) < 16, lse, delta)
        s_s[ch] = folded(stats)
        exchange(s_s.at[ch], s_r.at[ch], A_S + ch)
        stat_t[ch] = jnp.transpose(stats)

    def rows_of(table, p):
        lse = [table[pl.ds(p + HD * e, 1), :] for e in range(2)]
        delta = [table[pl.ds(p + HD * e + 16, 1), :] for e in range(2)]
        return lse, delta

    def far_backward(ch, p, carry):
        at = pair_at(p)
        here = pair_at(p - ch * CP)
        gq, gk, gv = backward_pair(
            qf[:, at], kf[:, at], vf[:, at], df[:, at],
            lambda e, scores: jnp.exp2(scores + bias_col[...]), *rows_of(far_t, p - ch * CP),
        )
        qk_s[ch, :, :, here] = joined(gq, gk)
        vf[:, at] = gv.astype(BF16)
        return carry

    def back_chunk(ch):
        cols, low, high = columns(ch)
        arrived(s_r.at[ch], A_S + ch)
        far_t[...] = jnp.transpose(unfolded(s_r[ch]))
        departed(qk_s.at[ch], A_QK + ch)
        lax.fori_loop(ch * CP, (ch + 1) * CP, functools.partial(far_backward, ch), 0)
        exchange(qk_s.at[ch], g_r.at[ch], A_G + ch)
        gv_s[ch] = joined(vf[:, low], vf[:, high])
        exchange(gv_s.at[ch], gv_r.at[ch], A_GV + ch)

    far_chunk(0)
    for step in range(1, NX):
        wx[step - 1].wait_recv()
        there = line_of(lax.rem(x + NX - step, NX), c)
        wc.append(send_w(w_full.at[there], w_full.at[there], wc_recv.at[step], sibling))
    for copy in wc:
        copy.wait_recv()
    arrived(go_r, A_GO)
    gf[:, : WIDTH // 2], gf[:, WIDTH // 2 :] = parted(go_r[...])
    for ch in range(CH):
        cols = pl.ds(ch * CW, CW)
        dp[:, cols] = nt(gp[...], w_full[cols, :]).astype(BF16)
        df[:, cols] = nt(gf[...], w_full[cols, :]).astype(BF16)
    for ch in range(1, CH):
        far_chunk(ch)
        combine_chunk(ch - 1)
    back_chunk(0)
    combine_chunk(CH - 1)

    for step in range(NX):
        to = lax.rem(x + step + 1, NX)
        c_s[step] = nn(attn_t[line_of(to, 1 - c), :], gp[...]).astype(BF16)
        send_r(c_s.at[step], c_r.at[step], rc_recv.at[step], sibling)
    for ch in range(1, CH):
        back_chunk(ch)

    ahead = []
    for step in range(NX):
        to = lax.rem(x + step + 1, NX)
        r_started[step].wait_recv()
        total = nn(attn_t[line_of(to, c), :], gp[...]) + c_r[step].astype(F32)
        if step < NX - 1:
            x_s[step] = total.astype(BF16)
            ahead.append(send_r(x_s.at[step], x_r.at[step], rx_recv.at[step], device(to, c, y, z)))
        else:
            own[...] = total

    def near_backward(ch, p, carry):
        at = pair_at(p)

        def masked(e, scores):
            return jnp.where(lax.bitwise_and(x_bwd[...], bits(p, e)) == 0, jnp.exp2(scores), 0.0)

        nq[:, at], nk[:, at], nv[:, at] = backward_pair(
            qp[:, at], kp[:, at], vp[:, at], dp[:, at], masked, *rows_of(stat_t.at[ch], p - ch * CP)
        )
        return carry

    def near_back_chunk(ch):
        lax.fori_loop(ch * CP, (ch + 1) * CP, functools.partial(near_backward, ch), 0)

    for ch in range(CH - 1):
        near_back_chunk(ch)
    for copy in ahead:
        copy.wait_recv()
    total = own[...]
    for step in range(NX - 1):
        total = total + x_r[step].astype(F32)
    y_s[...] = total.reshape(NY, BLOCK, WIDTH)
    ahead = []
    for step in range(NY - 1):
        to = lax.rem(y + step + 1, NY)
        ahead.append(send_r(y_s.at[to], y_r.at[step], ry_recv.at[step], device(x, c, to, z)))
    near_back_chunk(CH - 1)
    for copy in ahead:
        copy.wait_recv()
    total = y_s[y]
    for step in range(NY - 1):
        total = total + y_r[step]
    z_s[...] = tn(unfold(), stacked(total).astype(BF16)).astype(BF16).reshape(NZ, PACK, PAIR)
    ahead = []
    for step in range(NZ - 1):
        to = lax.rem(z + step + 1, NZ)
        ahead.append(send_r(z_s.at[to], z_r.at[step], rz_recv.at[step], device(x, c, y, to)))

    for ch in range(CH):
        cols = pl.ds(ch * CW, CW)
        done = nn(attn[...], w_full[:, cols]).astype(BF16)
        out_lo[:, cols] = nn(back, done).astype(BF16)

    for ch in range(CH):
        cols, low, high = pl.ds(ch * CW, CW), pl.ds(ch * CW, HW), pl.ds(ch * CW + HW, HW)
        arrived(g_r.at[ch], A_G + ch)
        far_q, far_k = parted(g_r[ch])
        out_q[:, cols] = nn(back, (nq[:, cols] + far_q.astype(F32)).astype(BF16)).astype(BF16)
        out_k[:, cols] = nn(back, (nk[:, cols] + far_k.astype(F32)).astype(BF16)).astype(BF16)
        arrived(gv_r.at[ch], A_GV + ch)
        far_low, far_high = parted(gv_r[ch])
        out_v[:, low] = nn(back, (nv[:, low] + far_low.astype(F32)).astype(BF16)).astype(BF16)
        out_v[:, high] = nn(back, (nv[:, high] + far_high.astype(F32)).astype(BF16)).astype(BF16)

    for copy in ahead:
        copy.wait_recv()
    total = z_s[z].astype(F32)
    for step in range(NZ - 1):
        total = total + z_r[step].astype(F32)
    for n in range(CHUNKS):
        out_w[:, n * PAIR : (n + 1) * PAIR] = total[n * ROWS : (n + 1) * ROWS] * factor
    for copy in w_started + r_started:
        copy.wait_send()
    for ch in range(CH):
        departed(v_s.at[ch], A_O + ch)
        departed(qk_s.at[ch], A_G + ch)
        departed(gv_s.at[ch], A_GV + ch)
        departed(l_s.at[ch], A_L + ch)
        departed(s_s.at[ch], A_S + ch)
    departed(go_s, A_GO)


def layer(queries, key_rows, value_rows, tissue, segment_len, dilation, out_weight, grad_out):
    shape = (TILES, WIDTH)
    vmem = pl.BlockSpec(memory_space=pltpu.VMEM)
    smem = pl.BlockSpec(memory_space=pltpu.SMEM)
    low, wide = pltpu.VMEM(shape, BF16), pltpu.VMEM(shape, F32)
    stats = pltpu.VMEM((CH, NS, 1, PAIR), F32)
    table = pltpu.VMEM((PAIR, TILES), F32)
    square = pltpu.VMEM((TILES, TILES), jnp.int32)
    both = pltpu.VMEM((CH, NS, 2 * EACH, CW), BF16)
    single = pltpu.VMEM((CH, NS, 2 * EACH, HW), BF16)
    ends = pltpu.VMEM((NS, 2 * EACH, WIDTH // 2), BF16)
    dma = pltpu.SemaphoreType.DMA
    factor = 1.0 / math.sqrt(NX * NC * NS * TILES)
    outs = pl.pallas_call(
        functools.partial(kernel, factor),
        out_shape=[jax.ShapeDtypeStruct(shape, BF16)] * 4 + [jax.ShapeDtypeStruct((ROWS, WIDTH), F32)],
        in_specs=[vmem] * 5 + [smem] * 2 + [vmem],
        out_specs=[vmem] * 5,
        scratch_shapes=[low] * 11 + [wide] + [low, pltpu.VMEM((WIDTH, TILES), BF16)] + [wide] * 3
        + [square] * 2 + [pltpu.VMEM((CH, TILES, PAIR), F32), pltpu.VMEM((CH, PAIR, TILES), F32), table]
        + [pltpu.VMEM((8, TILES), F32), pltpu.VMEM((TILES, TILES), F32)]
        + [both, single, single, both, single, single, both, single, ends, ends]
        + [stats] * 4
        + [
            pltpu.VMEM((16, WIDTH), BF16),
            pltpu.VMEM((PACK, PAIR), BF16),
            pltpu.VMEM((NZ, PACK, PAIR), BF16),
            pltpu.VMEM((WIDTH, WIDTH), BF16),
            pltpu.VMEM((NX, LINE, WIDTH), BF16),
            pltpu.VMEM((NX, LINE, WIDTH), BF16),
            pltpu.VMEM((LINE, WIDTH), F32),
            pltpu.VMEM((NX - 1, LINE, WIDTH), BF16),
            pltpu.VMEM((NX - 1, LINE, WIDTH), BF16),
            pltpu.VMEM((NY, BLOCK, WIDTH), F32),
            pltpu.VMEM((NY - 1, BLOCK, WIDTH), F32),
            pltpu.VMEM((NZ, PACK, PAIR), BF16),
            pltpu.VMEM((NZ - 1, PACK, PAIR), BF16),
            dma((A_ALL,)),
            dma((A_ALL,)),
            dma((NZ + NY + 2 * NX,)),
            dma((NZ,)),
            dma((NY,)),
            dma((NX,)),
            dma((NX,)),
            dma((NZ + NY + 2 * NX,)),
            dma((NX,)),
            dma((NX,)),
            dma((NY,)),
            dma((NZ,)),
        ],
        compiler_params=pltpu.CompilerParams(
            collective_id=0, has_side_effects=True, vmem_limit_bytes=60 * 1024 * 1024
        ),
    )(
        queries[0], key_rows[0], value_rows[0], grad_out[0], tissue, segment_len, dilation, out_weight
    )
    return tuple(out[None] for out in outs[:4]) + (outs[4],)


def solution(mesh):
    tiles = P("slide", "seq", None)
    rows = P(("slide", "seq"), None)
    return jax.shard_map(
        layer,
        mesh=mesh,
        in_specs=(tiles, tiles, tiles, P("slide", "seq"), P(), P(), rows, tiles),
        out_specs=(tiles, tiles, tiles, tiles, rows),
        check_vma=False,
    )
```

```python
import functools
import math

import jax
import jax.numpy as jnp
from jax import lax
from jax.experimental import pallas as pl
from jax.experimental.pallas import tpu as pltpu
from jax.sharding import PartitionSpec as P

HD = 64
PAIR = 2 * HD
NX, NC, NY, NZ = 4, 2, 4, 8
NS = NY * NZ
TILES = 256
WIDTH = 1536
EACH = TILES // NS
PAIRS = WIDTH // PAIR
CH = 3
CW = WIDTH // CH
HW = CW // 2
CP = PAIRS // CH
LINE = WIDTH // (NX * NC)
BLOCK = LINE // NY
ROWS = BLOCK // NZ
CHUNKS = WIDTH // PAIR
PACK = 80
FLAG = 100.0
LOG2E = 1.4426950408889634
SCALE = HD**-0.5
NONE = -1e30
FLOOR = -1e29
MESH = pl.DeviceIdType.MESH
F32 = jnp.float32
BF16 = jnp.bfloat16
A_QK, A_V, A_O, A_G, A_GV, A_L, A_S = (CH * n for n in range(7))
A_GO = 7 * CH
A_ALL = 7 * CH + 1
SLOTS = PAIR // EACH


def nt(a, b):
    return lax.dot_general(a, b, (((1,), (1,)), ((), ())), preferred_element_type=F32)


def nn(a, b):
    return lax.dot_general(a, b, (((1,), (0,)), ((), ())), preferred_element_type=F32)


def tn(a, b):
    return lax.dot_general(a, b, (((0,), (0,)), ((), ())), preferred_element_type=F32)


def doubled(value):
    high = value.astype(BF16)
    return jnp.concatenate([high, (value - high.astype(F32)).astype(BF16)], axis=1)


def tripled(value):
    high = value.astype(BF16)
    rest = value - high.astype(F32)
    middle = rest.astype(BF16)
    return jnp.concatenate([high, middle, (rest - middle.astype(F32)).astype(BF16)], axis=1)


def slot_lane(lane):
    slot = lax.rem(lane, SLOTS)
    inner = lax.rem(slot, SLOTS // 2)
    return lax.div(inner, 2) + HD * lax.rem(inner, 2) + 16 * lax.div(slot, SLOTS // 2)


def own_slots():
    shape = (TILES, PAIR)
    return lax.div(iota(shape, 1), SLOTS) == lax.rem(iota(shape, 0), EACH)


def folded(stats):
    tall = (3 * PAIR, PAIR)
    move = (lax.rem(iota(tall, 0), PAIR) == slot_lane(iota(tall, 1))).astype(F32).astype(BF16)
    spread = jnp.where(own_slots(), nn(tripled(stats), move), 0.0)
    return jnp.sum(spread.reshape(NS, EACH, PAIR), axis=1, keepdims=True)


def unfolded(rows):
    tall = (3 * PAIR, PAIR)
    move = (slot_lane(lax.rem(iota(tall, 0), PAIR)) == iota(tall, 1)).astype(F32).astype(BF16)
    spread = jnp.broadcast_to(rows, (NS, EACH, PAIR)).reshape(TILES, PAIR)
    return nn(tripled(jnp.where(own_slots(), spread, 0.0)), move)


def iota(shape, axis):
    return lax.broadcasted_iota(jnp.int32, shape, axis)


def halves():
    low = (iota((1, PAIR), 1) < HD).astype(F32)
    return low.astype(BF16), (1.0 - low).astype(BF16)


def joined(a, b):
    shape = (NS, EACH, a.shape[1])
    both = [a.astype(F32).reshape(shape), b.astype(F32).reshape(shape)]
    return jnp.concatenate(both, axis=1).astype(BF16)


def parted(block):
    wide = block.astype(F32)
    shape = (TILES, block.shape[2])
    return wide[:, :EACH].reshape(shape).astype(BF16), wide[:, EACH:].reshape(shape).astype(BF16)


def unfold():
    line = iota((CHUNKS * BLOCK, PAIR), 0)
    inner = lax.rem(line, BLOCK)
    want = lax.div(inner, ROWS) * PACK + lax.div(line, BLOCK) * ROWS + lax.rem(inner, ROWS)
    lane = iota((CHUNKS * BLOCK, PAIR), 1)
    parts = [(lane + PAIR * n == want).astype(F32).astype(BF16) for n in range(NZ * PACK // PAIR)]
    return jnp.concatenate(parts, axis=1)


def stacked(value):
    return jnp.concatenate([value[:, n * PAIR : (n + 1) * PAIR] for n in range(CHUNKS)], axis=0)


def pair_at(p):
    return pl.ds(pl.multiple_of(p * PAIR, PAIR), PAIR)


def forward_pair(q, k, v, masked):
    ones = halves()
    tops, sums = [], []
    for e in range(2):
        scores = masked(e, nt(q * ones[e], k) * (SCALE * LOG2E))
        top = jnp.maximum(jnp.max(scores, axis=1, keepdims=True), FLOOR)
        weights = jnp.exp2(scores - top).astype(BF16)
        tops.append(top)
        sums.append(nn(weights, v * ones[e] + ones[1 - e]))
    low = iota((TILES, PAIR), 1) < HD
    total = pltpu.roll(jnp.where(low, sums[1], sums[0]), HD, 1)
    total = jnp.maximum(total, 1e-30)
    out = jnp.where(low, sums[0], sums[1]) / total
    lse = jnp.where(low, tops[0], tops[1]) + jnp.log(total) * LOG2E
    return out, lse


def backward_pair(q, k, v, d, masked, lse, delta):
    ones = halves()
    gq = gk = gv = None
    for e in range(2):
        qe, de, ke = q * ones[e], d * ones[e], k * ones[e]
        probs = masked(e, nt(k, qe) * (SCALE * LOG2E) - lse[e])
        dscore = (probs * (nt(v, de) - delta[e])).astype(BF16)
        terms = (tn(dscore, ke), nn(dscore, qe), nn(probs.astype(BF16), de))
        gq, gk, gv = terms if e == 0 else (gq + terms[0], gk + terms[1], gv + terms[2])
    return gq * SCALE, gk * SCALE, gv


def remote(src, dst, send, recv, peer):
    return pltpu.make_async_remote_copy(
        src_ref=src, dst_ref=dst, send_sem=send, recv_sem=recv, device_id=peer, device_id_type=MESH
    )


def kernel(
    factor,
    q_in, k_in, v_in, g_in, keep_in, seg, dil, w_in,
    out_lo, out_q, out_k, out_v, out_w,
    qp, kp, vp, gp, dp, qf, kf, vf, gf, df, of, o_near, attn, attn_t, nq, nk, nv,
    x_fwd, x_bwd, stat, stat_t, far_t, bias_row, bias_col,
    qk_s, v_s, gv_s, qk_r, v_r, o_r, g_r, gv_r, go_s, go_r,
    l_s, l_r, s_s, s_r,
    w_pad, w_src, w_z, w_full,
    c_s, c_r, own, x_s, x_r, y_s, y_r, z_s, z_r,
    a_send, a_recv, w_send, wz_recv, wy_recv, wx_recv, wc_recv,
    r_send, rc_recv, rx_recv, ry_recv, rz_recv,
):
    slide = lax.axis_index("slide")
    me = lax.axis_index("seq")
    x, c = lax.div(slide, NC), lax.rem(slide, NC)
    y, z = lax.div(me, NZ), lax.rem(me, NZ)

    def device(xx, cc, yy, zz):
        return (xx * NC + cc, yy * NZ + zz)

    def peer_of(n):
        return lax.rem(y + lax.div(n, NZ), NY) * NZ + lax.rem(z + lax.rem(n, NZ), NZ)

    sibling = device(x, 1 - c, y, z)
    barrier = pltpu.get_barrier_semaphore()

    def greet(n, carry):
        pl.semaphore_signal(barrier, inc=1, device_id=(slide, peer_of(n)), device_id_type=MESH)
        return carry

    lax.fori_loop(1, NS, greet, 0)
    for peer in [sibling] + [device(lax.rem(x + step, NX), c, y, z) for step in range(1, NX)]:
        pl.semaphore_signal(barrier, inc=1, device_id=peer, device_id_type=MESH)

    def exchange(src, dst, k):
        def body(n, carry):
            peer = peer_of(n)
            remote(src.at[peer], dst.at[me], a_send.at[k], a_recv.at[k], (slide, peer)).start()
            return carry

        lax.fori_loop(1, NS, body, 0)
        dst.at[me][...] = src.at[me][...]

    def arrived(dst, k):
        part = dst.at[pl.ds(0, NS - 1)]
        pltpu.make_async_copy(part, part, a_recv.at[k]).wait()

    def departed(src, k):
        part = src.at[pl.ds(0, NS - 1)]
        pltpu.make_async_copy(part, part, a_send.at[k]).wait()

    w_started, r_started = [], []

    def send_w(src, dst, recv, peer):
        copy = remote(src, dst, w_send.at[len(w_started)], recv, peer)
        copy.start()
        w_started.append(copy)
        return copy

    def send_r(src, dst, recv, peer):
        copy = remote(src, dst, r_send.at[len(r_started)], recv, peer)
        copy.start()
        r_started.append(copy)
        return copy

    def line_of(xx, cc):
        return pl.ds(pl.multiple_of((xx * NC + cc) * LINE, 16), LINE)

    square = (TILES, TILES)
    line, lane = iota(square, 0), iota(square, 1)
    order = (lane == lax.rem(line, EACH) * NS + lax.div(line, EACH)).astype(F32).astype(BF16)
    keep = keep_in[...].astype(F32).astype(BF16)
    keep_cols = nt(order, jnp.broadcast_to(keep, (PAIR, TILES)))
    keep_wide = jnp.concatenate([keep_cols] * (CW // PAIR), axis=1) > 0.5
    for ch in range(CH):
        cols = pl.ds(ch * CW, CW)
        q = nn(order, q_in[:, cols])
        k = nn(order, k_in[:, cols])
        qk_s[ch] = joined(q, jnp.where(keep_wide, k, FLAG))
        if ch == 0:
            pl.semaphore_wait(barrier, NS - 1 + NX)
        exchange(qk_s.at[ch], qk_r.at[ch], A_QK + ch)
        if ch == 0:
            w_pad[...] = jnp.zeros_like(w_pad)
            w_pad[0:ROWS, :] = w_in[...]
            out_row, in_row = iota((PACK, CHUNKS * 16), 0), iota((PACK, CHUNKS * 16), 1)
            chosen = (lax.div(out_row, ROWS) == lax.div(in_row, 16)) & (lax.rem(out_row, ROWS) == lax.rem(in_row, 16))
            w_src[...] = nn(chosen.astype(F32).astype(BF16), stacked(w_pad[...])).astype(BF16)
            w_z[z] = w_src[...]
            wz = [
                send_w(w_src, w_z.at[z], wz_recv.at[step - 1], device(x, c, y, lax.rem(z + step, NZ)))
                for step in range(1, NZ)
            ]
        qp[:, cols] = q.astype(BF16)
        kp[:, cols] = k.astype(BF16)
        v = nn(order, v_in[:, cols])
        v_s[ch] = joined(v[:, :HW], v[:, HW:])
        exchange(v_s.at[ch], v_r.at[ch], A_V + ch)
        vp[:, cols] = v.astype(BF16)
        if ch == 0:
            half = WIDTH // 2
            ends = []
            for cols in (pl.ds(0, half), pl.ds(half, half)):
                ends.append(nn(order, g_in[:, cols]))
                gp[:, cols] = ends[-1].astype(BF16)
            go_s[...] = joined(*ends)
            exchange(go_s, go_r, A_GO)

    keep_row = nt(jnp.broadcast_to(keep, (16, TILES)), order)[0:1]
    pos_l = lax.rem(line, EACH) * NS + lax.div(line, EACH)
    pos_c = lax.rem(lane, EACH) * NS + lax.div(lane, EACH)
    apart = lax.bitwise_xor(pos_l, pos_c)
    same = line == lane
    x_fwd[...] = jnp.where(same, 0, apart + jnp.where(keep_row > 0.5, 0, 65536))
    x_bwd[...] = jnp.where(same, 0, apart + jnp.where(keep_wide[:, :TILES], 0, 65536))

    def bits(p, e):
        head = 2 * p + e
        return 65536 + (TILES - seg[head]) + (dil[head] - 1)

    for copy in wz:
        copy.wait_recv()
    mine = pl.ds(pl.multiple_of(((x * NC + c) * NY + y) * BLOCK, 16), BLOCK)
    rows = nn(unfold(), w_z[...].reshape(NZ * PACK, PAIR)).astype(BF16)
    for n in range(CHUNKS):
        w_full[mine, n * PAIR : (n + 1) * PAIR] = rows[n * BLOCK : (n + 1) * BLOCK]
    wy = [
        send_w(w_full.at[mine], w_full.at[mine], wy_recv.at[step - 1], device(x, c, lax.rem(y + step, NY), z))
        for step in range(1, NY)
    ]

    def put_stat(p, stats, values):
        return jnp.where(lax.rem(iota((TILES, PAIR), 1), HD) == p, values, stats)

    def near_forward(ch, p, stats):
        at = pair_at(p)

        def masked(e, scores):
            return jnp.where(lax.bitwise_and(x_fwd[...], bits(p, e)) == 0, scores, NONE)

        out, lse = forward_pair(qp[:, at], kp[:, at], vp[:, at], masked)
        o_near[:, at] = out
        return put_stat(p - ch * CP, stats, lse)

    def near_chunk(ch):
        empty = jnp.zeros((TILES, PAIR), F32)
        stat[ch] = lax.fori_loop(ch * CP, (ch + 1) * CP, functools.partial(near_forward, ch), empty)

    near_chunk(0)

    for copy in wy:
        copy.wait_recv()
    mine = line_of(x, c)
    wx = [
        send_w(w_full.at[mine], w_full.at[mine], wx_recv.at[step - 1], device(lax.rem(x + step, NX), c, y, z))
        for step in range(1, NX)
    ]
    wc = [send_w(w_full.at[mine], w_full.at[mine], wc_recv.at[0], sibling)]
    for ch in range(1, CH):
        near_chunk(ch)

    def columns(ch):
        return pl.ds(ch * CW, CW), pl.ds(ch * CW, HW), pl.ds(ch * CW + HW, HW)

    def far_forward(ch, p, stats):
        at = pair_at(p)
        out, lse = forward_pair(
            qf[:, at], kf[:, at], vf[:, at], lambda e, scores: scores + bias_row[0:1, :]
        )
        of[:, at] = out.astype(BF16)
        return put_stat(p - ch * CP, stats, lse)

    def far_chunk(ch):
        cols, low, high = columns(ch)
        arrived(qk_r.at[ch], A_QK + ch)
        qf[:, cols], kf[:, cols] = parted(qk_r[ch])
        if ch == 0:
            bias = jnp.where(kf[:, 0:PAIR].astype(F32) > FLAG / 2, NONE, 0.0)
            bias_col[...] = jnp.concatenate([bias, bias], axis=1)
            bias_row[...] = jnp.transpose(bias)[0:8]
        arrived(v_r.at[ch], A_V + ch)
        vf[:, low], vf[:, high] = parted(v_r[ch])
        empty = jnp.zeros((TILES, PAIR), F32)
        lse = lax.fori_loop(ch * CP, (ch + 1) * CP, functools.partial(far_forward, ch), empty)
        departed(v_s.at[ch], A_V + ch)
        v_s[ch] = joined(of[:, low], of[:, high])
        exchange(v_s.at[ch], o_r.at[ch], A_O + ch)
        l_s[ch] = folded(lse)
        exchange(l_s.at[ch], l_r.at[ch], A_L + ch)

    def combine(ch, share_near, share_far, p, delta):
        at = pair_at(p)
        near = p - ch * CP
        tall = (2 * PAIR, PAIR)
        first, second = lax.rem(iota(tall, 0), PAIR), iota(tall, 1)
        together = (first < HD) == (second < HD)
        spread = (together & (lax.rem(first, HD) == near)).astype(F32).astype(BF16)
        gather = (together & (lax.rem(second, HD) == near + 16)).astype(F32).astype(BF16)
        far = of[:, at].astype(F32)
        whole = nn(share_near, spread) * o_near[:, at] + nn(share_far, spread) * far
        attn[:, at] = whole.astype(BF16)
        attn_t[at, :] = jnp.transpose(whole).astype(BF16)
        return delta + nn(doubled(whole * dp[:, at].astype(F32)), gather)

    def combine_chunk(ch):
        cols, low, high = columns(ch)
        arrived(l_r.at[ch], A_L + ch)
        lse_near = stat[ch]
        lse_far = unfolded(l_r[ch])
        top = jnp.maximum(lse_near, lse_far)
        lse = top + jnp.log(jnp.exp2(lse_near - top) + jnp.exp2(lse_far - top)) * LOG2E
        share_near = doubled(jnp.exp2(lse_near - lse))
        share_far = doubled(jnp.exp2(lse_far - lse))
        arrived(o_r.at[ch], A_O + ch)
        of[:, low], of[:, high] = parted(o_r[ch])
        body = functools.partial(combine, ch, share_near, share_far)
        delta = lax.fori_loop(ch * CP, (ch + 1) * CP, body, jnp.zeros((TILES, PAIR), F32))
        stats = jnp.where(lax.rem(iota((TILES, PAIR), 1), HD) < 16, lse, delta)
        s_s[ch] = folded(stats)
        exchange(s_s.at[ch], s_r.at[ch], A_S + ch)
        stat_t[ch] = jnp.transpose(stats)

    def rows_of(table, p):
        lse = [table[pl.ds(p + HD * e, 1), :] for e in range(2)]
        delta = [table[pl.ds(p + HD * e + 16, 1), :] for e in range(2)]
        return lse, delta

    def far_backward(ch, p, carry):
        at = pair_at(p)
        here = pair_at(p - ch * CP)
        gq, gk, gv = backward_pair(
            qf[:, at], kf[:, at], vf[:, at], df[:, at],
            lambda e, scores: jnp.exp2(scores + bias_col[...]), *rows_of(far_t, p - ch * CP),
        )
        qk_s[ch, :, :, here] = joined(gq, gk)
        vf[:, at] = gv.astype(BF16)
        return carry

    def back_chunk(ch):
        cols, low, high = columns(ch)
        arrived(s_r.at[ch], A_S + ch)
        far_t[...] = jnp.transpose(unfolded(s_r[ch]))
        departed(qk_s.at[ch], A_QK + ch)
        lax.fori_loop(ch * CP, (ch + 1) * CP, functools.partial(far_backward, ch), 0)
        exchange(qk_s.at[ch], g_r.at[ch], A_G + ch)
        gv_s[ch] = joined(vf[:, low], vf[:, high])
        exchange(gv_s.at[ch], gv_r.at[ch], A_GV + ch)

    far_chunk(0)
    for step in range(1, NX):
        wx[step - 1].wait_recv()
        there = line_of(lax.rem(x + NX - step, NX), c)
        wc.append(send_w(w_full.at[there], w_full.at[there], wc_recv.at[step], sibling))
    for copy in wc:
        copy.wait_recv()
    arrived(go_r, A_GO)
    gf[:, : WIDTH // 2], gf[:, WIDTH // 2 :] = parted(go_r[...])
    for ch in range(CH):
        cols = pl.ds(ch * CW, CW)
        dp[:, cols] = nt(gp[...], w_full[cols, :]).astype(BF16)
        df[:, cols] = nt(gf[...], w_full[cols, :]).astype(BF16)
    for ch in range(1, CH):
        far_chunk(ch)
        combine_chunk(ch - 1)
    back_chunk(0)
    combine_chunk(CH - 1)

    for step in range(NX):
        to = lax.rem(x + step + 1, NX)
        c_s[step] = nn(attn_t[line_of(to, 1 - c), :], gp[...]).astype(BF16)
        send_r(c_s.at[step], c_r.at[step], rc_recv.at[step], sibling)
    for ch in range(1, CH - 1):
        back_chunk(ch)

    ahead = []
    for step in range(NX):
        to = lax.rem(x + step + 1, NX)
        r_started[step].wait_recv()
        total = nn(attn_t[line_of(to, c), :], gp[...]) + c_r[step].astype(F32)
        if step < NX - 1:
            x_s[step] = total.astype(BF16)
            ahead.append(send_r(x_s.at[step], x_r.at[step], rx_recv.at[step], device(to, c, y, z)))
        else:
            own[...] = total
    back_chunk(CH - 1)

    def near_backward(ch, p, carry):
        at = pair_at(p)

        def masked(e, scores):
            return jnp.where(lax.bitwise_and(x_bwd[...], bits(p, e)) == 0, jnp.exp2(scores), 0.0)

        nq[:, at], nk[:, at], nv[:, at] = backward_pair(
            qp[:, at], kp[:, at], vp[:, at], dp[:, at], masked, *rows_of(stat_t.at[ch], p - ch * CP)
        )
        return carry

    def near_back_chunk(ch):
        lax.fori_loop(ch * CP, (ch + 1) * CP, functools.partial(near_backward, ch), 0)

    near_back_chunk(0)
    for copy in ahead:
        copy.wait_recv()
    total = own[...]
    for step in range(NX - 1):
        total = total + x_r[step].astype(F32)
    y_s[...] = total.reshape(NY, BLOCK, WIDTH)
    ahead = []
    for step in range(NY - 1):
        to = lax.rem(y + step + 1, NY)
        ahead.append(send_r(y_s.at[to], y_r.at[step], ry_recv.at[step], device(x, c, to, z)))
    for ch in range(1, CH):
        near_back_chunk(ch)
    for copy in ahead:
        copy.wait_recv()
    total = y_s[y]
    for step in range(NY - 1):
        total = total + y_r[step]
    z_s[...] = tn(unfold(), stacked(total).astype(BF16)).astype(BF16).reshape(NZ, PACK, PAIR)
    ahead = []
    for step in range(NZ - 1):
        to = lax.rem(z + step + 1, NZ)
        ahead.append(send_r(z_s.at[to], z_r.at[step], rz_recv.at[step], device(x, c, y, to)))

    for ch in range(CH):
        cols = pl.ds(ch * CW, CW)
        done = nn(attn[...], w_full[:, cols]).astype(BF16)
        out_lo[:, cols] = done

    for ch in range(CH):
        cols, low, high = pl.ds(ch * CW, CW), pl.ds(ch * CW, HW), pl.ds(ch * CW + HW, HW)
        arrived(g_r.at[ch], A_G + ch)
        far_q, far_k = parted(g_r[ch])
        out_q[:, cols] = (nq[:, cols] + far_q.astype(F32)).astype(BF16)
        out_k[:, cols] = (nk[:, cols] + far_k.astype(F32)).astype(BF16)
        arrived(gv_r.at[ch], A_GV + ch)
        far_low, far_high = parted(gv_r[ch])
        out_v[:, low] = (nv[:, low] + far_low.astype(F32)).astype(BF16)
        out_v[:, high] = (nv[:, high] + far_high.astype(F32)).astype(BF16)

    for copy in ahead:
        copy.wait_recv()
    total = z_s[z].astype(F32)
    for step in range(NZ - 1):
        total = total + z_r[step].astype(F32)
    for n in range(CHUNKS):
        out_w[:, n * PAIR : (n + 1) * PAIR] = total[n * ROWS : (n + 1) * ROWS] * factor
    for copy in w_started + r_started:
        copy.wait_send()
    for ch in range(CH):
        departed(v_s.at[ch], A_O + ch)
        departed(qk_s.at[ch], A_G + ch)
        departed(gv_s.at[ch], A_GV + ch)
        departed(l_s.at[ch], A_L + ch)
        departed(s_s.at[ch], A_S + ch)
    departed(go_s, A_GO)


def reorder(*refs):
    square = (TILES, TILES)
    line, lane = iota(square, 0), iota(square, 1)
    back = (lane == lax.rem(line, NS) * EACH + lax.div(line, NS)).astype(F32).astype(BF16)
    for src, dst in zip(refs[:4], refs[4:]):
        dst[...] = nn(back, src[...]).astype(BF16)


def natural(rows):
    wide = WIDTH // 2
    block = pl.BlockSpec((TILES, wide), lambda n: (0, n))
    return pl.pallas_call(
        reorder,
        grid=(WIDTH // wide,),
        out_shape=[jax.ShapeDtypeStruct((TILES, WIDTH), BF16)] * 4,
        in_specs=[block] * 4,
        out_specs=[block] * 4,
    )(*rows)


def layer(queries, key_rows, value_rows, tissue, segment_len, dilation, out_weight, grad_out):
    shape = (TILES, WIDTH)
    vmem = pl.BlockSpec(memory_space=pltpu.VMEM)
    smem = pl.BlockSpec(memory_space=pltpu.SMEM)
    low, wide = pltpu.VMEM(shape, BF16), pltpu.VMEM(shape, F32)
    stats = pltpu.VMEM((CH, NS, 1, PAIR), F32)
    table = pltpu.VMEM((PAIR, TILES), F32)
    square = pltpu.VMEM((TILES, TILES), jnp.int32)
    both = pltpu.VMEM((CH, NS, 2 * EACH, CW), BF16)
    single = pltpu.VMEM((CH, NS, 2 * EACH, HW), BF16)
    ends = pltpu.VMEM((NS, 2 * EACH, WIDTH // 2), BF16)
    dma = pltpu.SemaphoreType.DMA
    factor = 1.0 / math.sqrt(NX * NC * NS * TILES)
    outs = pl.pallas_call(
        functools.partial(kernel, factor),
        out_shape=[jax.ShapeDtypeStruct(shape, BF16)] * 4 + [jax.ShapeDtypeStruct((ROWS, WIDTH), F32)],
        in_specs=[vmem] * 5 + [smem] * 2 + [vmem],
        out_specs=[vmem] * 5,
        scratch_shapes=[low] * 11 + [wide] + [low, pltpu.VMEM((WIDTH, TILES), BF16)] + [wide] * 3
        + [square] * 2 + [pltpu.VMEM((CH, TILES, PAIR), F32), pltpu.VMEM((CH, PAIR, TILES), F32), table]
        + [pltpu.VMEM((8, TILES), F32), pltpu.VMEM((TILES, TILES), F32)]
        + [both, single, single, both, single, single, both, single, ends, ends]
        + [stats] * 4
        + [
            pltpu.VMEM((16, WIDTH), BF16),
            pltpu.VMEM((PACK, PAIR), BF16),
            pltpu.VMEM((NZ, PACK, PAIR), BF16),
            pltpu.VMEM((WIDTH, WIDTH), BF16),
            pltpu.VMEM((NX, LINE, WIDTH), BF16),
            pltpu.VMEM((NX, LINE, WIDTH), BF16),
            pltpu.VMEM((LINE, WIDTH), F32),
            pltpu.VMEM((NX - 1, LINE, WIDTH), BF16),
            pltpu.VMEM((NX - 1, LINE, WIDTH), BF16),
            pltpu.VMEM((NY, BLOCK, WIDTH), F32),
            pltpu.VMEM((NY - 1, BLOCK, WIDTH), F32),
            pltpu.VMEM((NZ, PACK, PAIR), BF16),
            pltpu.VMEM((NZ - 1, PACK, PAIR), BF16),
            dma((A_ALL,)),
            dma((A_ALL,)),
            dma((NZ + NY + 2 * NX,)),
            dma((NZ,)),
            dma((NY,)),
            dma((NX,)),
            dma((NX,)),
            dma((NZ + NY + 2 * NX,)),
            dma((NX,)),
            dma((NX,)),
            dma((NY,)),
            dma((NZ,)),
        ],
        compiler_params=pltpu.CompilerParams(
            collective_id=0, has_side_effects=True, vmem_limit_bytes=60 * 1024 * 1024
        ),
    )(
        queries[0], key_rows[0], value_rows[0], grad_out[0], tissue, segment_len, dilation, out_weight
    )
    return tuple(out[None] for out in natural(outs[:4])) + (outs[4],)


def solution(mesh):
    tiles = P("slide", "seq", None)
    rows = P(("slide", "seq"), None)
    return jax.shard_map(
        layer,
        mesh=mesh,
        in_specs=(tiles, tiles, tiles, P("slide", "seq"), P(), P(), rows, tiles),
        out_specs=(tiles, tiles, tiles, tiles, rows),
        check_vma=False,
    )
```

```python
import functools
import math

import jax
import jax.numpy as jnp
from jax import lax
from jax.experimental import pallas as pl
from jax.experimental.pallas import tpu as pltpu
from jax.sharding import PartitionSpec as P

HD = 64
PAIR = 2 * HD
NX, NC, NY, NZ = 4, 2, 4, 8
NS = NY * NZ
TILES = 256
WIDTH = 1536
EACH = TILES // NS
PAIRS = WIDTH // PAIR
CH = 3
CW = WIDTH // CH
HW = CW // 2
CP = PAIRS // CH
LINE = WIDTH // (NX * NC)
BLOCK = LINE // NY
ROWS = BLOCK // NZ
CHUNKS = WIDTH // PAIR
PACK = 80
FLAG = 100.0
LOG2E = 1.4426950408889634
SCALE = HD**-0.5
NONE = -1e30
FLOOR = -1e29
MESH = pl.DeviceIdType.MESH
F32 = jnp.float32
BF16 = jnp.bfloat16
A_QK, A_O, A_G, A_L, A_S = (CH * n for n in range(5))
A_GO = 5 * CH
A_ALL = 5 * CH + 1
SLOTS = PAIR // EACH


def nt(a, b):
    return lax.dot_general(a, b, (((1,), (1,)), ((), ())), preferred_element_type=F32)


def nn(a, b):
    return lax.dot_general(a, b, (((1,), (0,)), ((), ())), preferred_element_type=F32)


def tn(a, b):
    return lax.dot_general(a, b, (((0,), (0,)), ((), ())), preferred_element_type=F32)


def doubled(value):
    high = value.astype(BF16)
    return jnp.concatenate([high, (value - high.astype(F32)).astype(BF16)], axis=1)


def tripled(value):
    high = value.astype(BF16)
    rest = value - high.astype(F32)
    middle = rest.astype(BF16)
    return jnp.concatenate([high, middle, (rest - middle.astype(F32)).astype(BF16)], axis=1)


def slot_lane(lane):
    slot = lax.rem(lane, SLOTS)
    inner = lax.rem(slot, SLOTS // 2)
    return lax.div(inner, 2) + HD * lax.rem(inner, 2) + 16 * lax.div(slot, SLOTS // 2)


def own_slots():
    shape = (TILES, PAIR)
    return lax.div(iota(shape, 1), SLOTS) == lax.rem(iota(shape, 0), EACH)


def folded(stats):
    tall = (3 * PAIR, PAIR)
    move = (lax.rem(iota(tall, 0), PAIR) == slot_lane(iota(tall, 1))).astype(F32).astype(BF16)
    spread = jnp.where(own_slots(), nn(tripled(stats), move), 0.0)
    return jnp.sum(spread.reshape(NS, EACH, PAIR), axis=1, keepdims=True)


def unfolded(rows):
    tall = (3 * PAIR, PAIR)
    move = (slot_lane(lax.rem(iota(tall, 0), PAIR)) == iota(tall, 1)).astype(F32).astype(BF16)
    spread = jnp.broadcast_to(rows, (NS, EACH, PAIR)).reshape(TILES, PAIR)
    return nn(tripled(jnp.where(own_slots(), spread, 0.0)), move)


def iota(shape, axis):
    return lax.broadcasted_iota(jnp.int32, shape, axis)


def halves():
    low = (iota((1, PAIR), 1) < HD).astype(F32)
    return low.astype(BF16), (1.0 - low).astype(BF16)


def joined(a, b):
    shape = (NS, EACH, a.shape[1])
    both = [a.astype(F32).reshape(shape), b.astype(F32).reshape(shape)]
    return jnp.concatenate(both, axis=1).astype(BF16)


def parted(block):
    wide = block.astype(F32)
    shape = (TILES, block.shape[2])
    return wide[:, :EACH].reshape(shape).astype(BF16), wide[:, EACH:].reshape(shape).astype(BF16)


def unfold():
    line = iota((CHUNKS * BLOCK, PAIR), 0)
    inner = lax.rem(line, BLOCK)
    want = lax.div(inner, ROWS) * PACK + lax.div(line, BLOCK) * ROWS + lax.rem(inner, ROWS)
    lane = iota((CHUNKS * BLOCK, PAIR), 1)
    parts = [(lane + PAIR * n == want).astype(F32).astype(BF16) for n in range(NZ * PACK // PAIR)]
    return jnp.concatenate(parts, axis=1)


def stacked(value):
    return jnp.concatenate([value[:, n * PAIR : (n + 1) * PAIR] for n in range(CHUNKS)], axis=0)


def pair_at(p):
    return pl.ds(pl.multiple_of(p * PAIR, PAIR), PAIR)


def forward_pair(q, k, v, masked):
    ones = halves()
    tops, sums = [], []
    for e in range(2):
        scores = masked(e, nt(q * ones[e], k) * (SCALE * LOG2E))
        top = jnp.maximum(jnp.max(scores, axis=1, keepdims=True), FLOOR)
        weights = jnp.exp2(scores - top).astype(BF16)
        tops.append(top)
        sums.append(nn(weights, v * ones[e] + ones[1 - e]))
    low = iota((TILES, PAIR), 1) < HD
    total = pltpu.roll(jnp.where(low, sums[1], sums[0]), HD, 1)
    total = jnp.maximum(total, 1e-30)
    out = jnp.where(low, sums[0], sums[1]) / total
    lse = jnp.where(low, tops[0], tops[1]) + jnp.log(total) * LOG2E
    return out, lse


def backward_pair(q, k, v, d, masked, lse, delta):
    ones = halves()
    gq = gk = gv = None
    for e in range(2):
        qe, de, ke = q * ones[e], d * ones[e], k * ones[e]
        probs = masked(e, nt(k, qe) * (SCALE * LOG2E) - lse[e])
        dscore = (probs * (nt(v, de) - delta[e])).astype(BF16)
        terms = (tn(dscore, ke), nn(dscore, qe), nn(probs.astype(BF16), de))
        gq, gk, gv = terms if e == 0 else (gq + terms[0], gk + terms[1], gv + terms[2])
    return gq * SCALE, gk * SCALE, gv


def remote(src, dst, send, recv, peer):
    return pltpu.make_async_remote_copy(
        src_ref=src, dst_ref=dst, send_sem=send, recv_sem=recv, device_id=peer, device_id_type=MESH
    )


def kernel(
    factor,
    q_in, k_in, v_in, g_in, keep_in, seg, dil, w_in,
    out_lo, out_q, out_k, out_v, out_w,
    qp, kp, vp, gp, dp, qf, kf, vf, gf, df, of, o_near, attn, attn_t, nq, nk, nv,
    x_fwd, x_bwd, stat, stat_t, far_t, bias_row, bias_col,
    qk_s, v_s, qk_r, o_r, g_r, go_s, go_r,
    l_s, l_r, s_s, s_r,
    w_pad, w_src, w_z, w_full,
    c_s, c_r, own, x_s, x_r, y_s, y_r, z_s, z_r,
    a_send, a_recv, w_send, wz_recv, wy_recv, wx_recv, wc_recv,
    r_send, rc_recv, rx_recv, ry_recv, rz_recv,
):
    slide = lax.axis_index("slide")
    me = lax.axis_index("seq")
    x, c = lax.div(slide, NC), lax.rem(slide, NC)
    y, z = lax.div(me, NZ), lax.rem(me, NZ)

    def device(xx, cc, yy, zz):
        return (xx * NC + cc, yy * NZ + zz)

    def peer_of(n):
        return lax.rem(y + lax.div(n, NZ), NY) * NZ + lax.rem(z + lax.rem(n, NZ), NZ)

    sibling = device(x, 1 - c, y, z)
    barrier = pltpu.get_barrier_semaphore()

    def greet(n, carry):
        pl.semaphore_signal(barrier, inc=1, device_id=(slide, peer_of(n)), device_id_type=MESH)
        return carry

    lax.fori_loop(1, NS, greet, 0)
    for peer in [sibling] + [device(lax.rem(x + step, NX), c, y, z) for step in range(1, NX)]:
        pl.semaphore_signal(barrier, inc=1, device_id=peer, device_id_type=MESH)

    def exchange(src, dst, k):
        def body(n, carry):
            peer = peer_of(n)
            remote(src.at[peer], dst.at[me], a_send.at[k], a_recv.at[k], (slide, peer)).start()
            return carry

        lax.fori_loop(1, NS, body, 0)
        dst.at[me][...] = src.at[me][...]

    def arrived(dst, k):
        part = dst.at[pl.ds(0, NS - 1)]
        pltpu.make_async_copy(part, part, a_recv.at[k]).wait()

    def departed(src, k):
        part = src.at[pl.ds(0, NS - 1)]
        pltpu.make_async_copy(part, part, a_send.at[k]).wait()

    w_started, r_started = [], []

    def send_w(src, dst, recv, peer):
        copy = remote(src, dst, w_send.at[len(w_started)], recv, peer)
        copy.start()
        w_started.append(copy)
        return copy

    def send_r(src, dst, recv, peer):
        copy = remote(src, dst, r_send.at[len(r_started)], recv, peer)
        copy.start()
        r_started.append(copy)
        return copy

    def line_of(xx, cc):
        return pl.ds(pl.multiple_of((xx * NC + cc) * LINE, 16), LINE)

    square = (TILES, TILES)
    line, lane = iota(square, 0), iota(square, 1)
    order = (lane == lax.rem(line, EACH) * NS + lax.div(line, EACH)).astype(F32).astype(BF16)
    keep = keep_in[...].astype(F32).astype(BF16)
    keep_cols = nt(order, jnp.broadcast_to(keep, (PAIR, TILES)))
    keep_wide = jnp.concatenate([keep_cols] * (CW // PAIR), axis=1) > 0.5
    for ch in range(CH):
        cols = pl.ds(ch * CW, CW)
        q = nn(order, q_in[:, cols])
        k = nn(order, k_in[:, cols])
        qk_s[ch, :, :, 0:CW] = joined(q, jnp.where(keep_wide, k, FLAG))
        v = nn(order, v_in[:, cols])
        qk_s[ch, :, :, CW:] = joined(v[:, :HW], v[:, HW:])
        if ch == 0:
            pl.semaphore_wait(barrier, NS - 1 + NX)
        exchange(qk_s.at[ch], qk_r.at[ch], A_QK + ch)
        if ch == 0:
            w_pad[...] = jnp.zeros_like(w_pad)
            w_pad[0:ROWS, :] = w_in[...]
            out_row, in_row = iota((PACK, CHUNKS * 16), 0), iota((PACK, CHUNKS * 16), 1)
            chosen = (lax.div(out_row, ROWS) == lax.div(in_row, 16)) & (lax.rem(out_row, ROWS) == lax.rem(in_row, 16))
            w_src[...] = nn(chosen.astype(F32).astype(BF16), stacked(w_pad[...])).astype(BF16)
            w_z[z] = w_src[...]
            wz = [
                send_w(w_src, w_z.at[z], wz_recv.at[step - 1], device(x, c, y, lax.rem(z + step, NZ)))
                for step in range(1, NZ)
            ]
        qp[:, cols] = q.astype(BF16)
        kp[:, cols] = k.astype(BF16)
        vp[:, cols] = v.astype(BF16)
        if ch == 0:
            half = WIDTH // 2
            ends = []
            for cols in (pl.ds(0, half), pl.ds(half, half)):
                ends.append(nn(order, g_in[:, cols]))
                gp[:, cols] = ends[-1].astype(BF16)
            go_s[...] = joined(*ends)
            exchange(go_s, go_r, A_GO)

    keep_row = nt(jnp.broadcast_to(keep, (16, TILES)), order)[0:1]
    pos_l = lax.rem(line, EACH) * NS + lax.div(line, EACH)
    pos_c = lax.rem(lane, EACH) * NS + lax.div(lane, EACH)
    apart = lax.bitwise_xor(pos_l, pos_c)
    same = line == lane
    x_fwd[...] = jnp.where(same, 0, apart + jnp.where(keep_row > 0.5, 0, 65536))
    x_bwd[...] = jnp.where(same, 0, apart + jnp.where(keep_wide[:, :TILES], 0, 65536))

    def bits(p, e):
        head = 2 * p + e
        return 65536 + (TILES - seg[head]) + (dil[head] - 1)

    for copy in wz:
        copy.wait_recv()
    mine = pl.ds(pl.multiple_of(((x * NC + c) * NY + y) * BLOCK, 16), BLOCK)
    rows = nn(unfold(), w_z[...].reshape(NZ * PACK, PAIR)).astype(BF16)
    for n in range(CHUNKS):
        w_full[mine, n * PAIR : (n + 1) * PAIR] = rows[n * BLOCK : (n + 1) * BLOCK]
    wy = [
        send_w(w_full.at[mine], w_full.at[mine], wy_recv.at[step - 1], device(x, c, lax.rem(y + step, NY), z))
        for step in range(1, NY)
    ]

    def put_stat(p, stats, values):
        return jnp.where(lax.rem(iota((TILES, PAIR), 1), HD) == p, values, stats)

    def near_forward(ch, p, stats):
        at = pair_at(p)

        def masked(e, scores):
            return jnp.where(lax.bitwise_and(x_fwd[...], bits(p, e)) == 0, scores, NONE)

        out, lse = forward_pair(qp[:, at], kp[:, at], vp[:, at], masked)
        o_near[:, at] = out
        return put_stat(p - ch * CP, stats, lse)

    def near_chunk(ch):
        empty = jnp.zeros((TILES, PAIR), F32)
        stat[ch] = lax.fori_loop(ch * CP, (ch + 1) * CP, functools.partial(near_forward, ch), empty)

    near_chunk(0)

    for copy in wy:
        copy.wait_recv()
    mine = line_of(x, c)
    wx = [
        send_w(w_full.at[mine], w_full.at[mine], wx_recv.at[step - 1], device(lax.rem(x + step, NX), c, y, z))
        for step in range(1, NX)
    ]
    wc = [send_w(w_full.at[mine], w_full.at[mine], wc_recv.at[0], sibling)]
    for ch in range(1, CH):
        near_chunk(ch)

    def columns(ch):
        return pl.ds(ch * CW, CW), pl.ds(ch * CW, HW), pl.ds(ch * CW + HW, HW)

    def far_forward(ch, p, stats):
        at = pair_at(p)
        out, lse = forward_pair(
            qf[:, at], kf[:, at], vf[:, at], lambda e, scores: scores + bias_row[0:1, :]
        )
        of[:, at] = out.astype(BF16)
        return put_stat(p - ch * CP, stats, lse)

    def far_chunk(ch):
        cols, low, high = columns(ch)
        arrived(qk_r.at[ch], A_QK + ch)
        qf[:, cols], kf[:, cols] = parted(qk_r[ch, :, :, 0:CW])
        if ch == 0:
            bias = jnp.where(kf[:, 0:PAIR].astype(F32) > FLAG / 2, NONE, 0.0)
            bias_col[...] = jnp.concatenate([bias, bias], axis=1)
            bias_row[...] = jnp.transpose(bias)[0:8]
        vf[:, low], vf[:, high] = parted(qk_r[ch, :, :, CW:])
        empty = jnp.zeros((TILES, PAIR), F32)
        lse = lax.fori_loop(ch * CP, (ch + 1) * CP, functools.partial(far_forward, ch), empty)
        v_s[ch] = joined(of[:, low], of[:, high])
        exchange(v_s.at[ch], o_r.at[ch], A_O + ch)
        l_s[ch] = folded(lse)
        exchange(l_s.at[ch], l_r.at[ch], A_L + ch)

    def combine(ch, share_near, share_far, p, delta):
        at = pair_at(p)
        near = p - ch * CP
        tall = (2 * PAIR, PAIR)
        first, second = lax.rem(iota(tall, 0), PAIR), iota(tall, 1)
        together = (first < HD) == (second < HD)
        spread = (together & (lax.rem(first, HD) == near)).astype(F32).astype(BF16)
        gather = (together & (lax.rem(second, HD) == near + 16)).astype(F32).astype(BF16)
        far = of[:, at].astype(F32)
        whole = nn(share_near, spread) * o_near[:, at] + nn(share_far, spread) * far
        attn[:, at] = whole.astype(BF16)
        attn_t[at, :] = jnp.transpose(whole).astype(BF16)
        return delta + nn(doubled(whole * dp[:, at].astype(F32)), gather)

    def combine_chunk(ch):
        cols, low, high = columns(ch)
        arrived(l_r.at[ch], A_L + ch)
        lse_near = stat[ch]
        lse_far = unfolded(l_r[ch])
        top = jnp.maximum(lse_near, lse_far)
        lse = top + jnp.log(jnp.exp2(lse_near - top) + jnp.exp2(lse_far - top)) * LOG2E
        share_near = doubled(jnp.exp2(lse_near - lse))
        share_far = doubled(jnp.exp2(lse_far - lse))
        arrived(o_r.at[ch], A_O + ch)
        of[:, low], of[:, high] = parted(o_r[ch])
        body = functools.partial(combine, ch, share_near, share_far)
        delta = lax.fori_loop(ch * CP, (ch + 1) * CP, body, jnp.zeros((TILES, PAIR), F32))
        stats = jnp.where(lax.rem(iota((TILES, PAIR), 1), HD) < 16, lse, delta)
        s_s[ch] = folded(stats)
        exchange(s_s.at[ch], s_r.at[ch], A_S + ch)
        stat_t[ch] = jnp.transpose(stats)

    def rows_of(table, p):
        lse = [table[pl.ds(p + HD * e, 1), :] for e in range(2)]
        delta = [table[pl.ds(p + HD * e + 16, 1), :] for e in range(2)]
        return lse, delta

    def far_backward(ch, p, carry):
        at = pair_at(p)
        here = pair_at(p - ch * CP)
        gq, gk, gv = backward_pair(
            qf[:, at], kf[:, at], vf[:, at], df[:, at],
            lambda e, scores: jnp.exp2(scores + bias_col[...]), *rows_of(far_t, p - ch * CP),
        )
        qk_s[ch, :, :, here] = joined(gq, gk)
        vf[:, at] = gv.astype(BF16)
        return carry

    def back_chunk(ch):
        cols, low, high = columns(ch)
        arrived(s_r.at[ch], A_S + ch)
        far_t[...] = jnp.transpose(unfolded(s_r[ch]))
        departed(qk_s.at[ch], A_QK + ch)
        lax.fori_loop(ch * CP, (ch + 1) * CP, functools.partial(far_backward, ch), 0)
        qk_s[ch, :, :, CW:] = joined(vf[:, low], vf[:, high])
        exchange(qk_s.at[ch], g_r.at[ch], A_G + ch)

    far_chunk(0)
    for step in range(1, NX):
        wx[step - 1].wait_recv()
        there = line_of(lax.rem(x + NX - step, NX), c)
        wc.append(send_w(w_full.at[there], w_full.at[there], wc_recv.at[step], sibling))
    far_chunk(1)
    for copy in wc:
        copy.wait_recv()
    arrived(go_r, A_GO)
    gf[:, : WIDTH // 2], gf[:, WIDTH // 2 :] = parted(go_r[...])
    for ch in range(CH):
        cols = pl.ds(ch * CW, CW)
        dp[:, cols] = nt(gp[...], w_full[cols, :]).astype(BF16)
        df[:, cols] = nt(gf[...], w_full[cols, :]).astype(BF16)
    combine_chunk(0)
    for ch in range(2, CH):
        far_chunk(ch)
        combine_chunk(ch - 1)
    back_chunk(0)
    combine_chunk(CH - 1)

    for step in range(NX):
        to = lax.rem(x + step + 1, NX)
        c_s[step] = nn(attn_t[line_of(to, 1 - c), :], gp[...]).astype(BF16)
        send_r(c_s.at[step], c_r.at[step], rc_recv.at[step], sibling)
    for ch in range(1, CH - 1):
        back_chunk(ch)

    ahead = []
    for step in range(NX):
        to = lax.rem(x + step + 1, NX)
        r_started[step].wait_recv()
        total = nn(attn_t[line_of(to, c), :], gp[...]) + c_r[step].astype(F32)
        if step < NX - 1:
            x_s[step] = total.astype(BF16)
            ahead.append(send_r(x_s.at[step], x_r.at[step], rx_recv.at[step], device(to, c, y, z)))
        else:
            own[...] = total
    back_chunk(CH - 1)

    def near_backward(ch, p, carry):
        at = pair_at(p)

        def masked(e, scores):
            return jnp.where(lax.bitwise_and(x_bwd[...], bits(p, e)) == 0, jnp.exp2(scores), 0.0)

        nq[:, at], nk[:, at], nv[:, at] = backward_pair(
            qp[:, at], kp[:, at], vp[:, at], dp[:, at], masked, *rows_of(stat_t.at[ch], p - ch * CP)
        )
        return carry

    def near_back_chunk(ch):
        lax.fori_loop(ch * CP, (ch + 1) * CP, functools.partial(near_backward, ch), 0)

    near_back_chunk(0)
    for copy in ahead:
        copy.wait_recv()
    total = own[...]
    for step in range(NX - 1):
        total = total + x_r[step].astype(F32)
    y_s[...] = total.reshape(NY, BLOCK, WIDTH)
    ahead = []
    for step in range(NY - 1):
        to = lax.rem(y + step + 1, NY)
        ahead.append(send_r(y_s.at[to], y_r.at[step], ry_recv.at[step], device(x, c, to, z)))
    for ch in range(1, CH):
        near_back_chunk(ch)
    for copy in ahead:
        copy.wait_recv()
    total = y_s[y]
    for step in range(NY - 1):
        total = total + y_r[step]
    z_s[...] = tn(unfold(), stacked(total).astype(BF16)).astype(BF16).reshape(NZ, PACK, PAIR)
    ahead = []
    for step in range(NZ - 1):
        to = lax.rem(z + step + 1, NZ)
        ahead.append(send_r(z_s.at[to], z_r.at[step], rz_recv.at[step], device(x, c, y, to)))

    for ch in range(CH):
        cols = pl.ds(ch * CW, CW)
        done = nn(attn[...], w_full[:, cols]).astype(BF16)
        out_lo[:, cols] = done

    for ch in range(CH):
        cols, low, high = pl.ds(ch * CW, CW), pl.ds(ch * CW, HW), pl.ds(ch * CW + HW, HW)
        arrived(g_r.at[ch], A_G + ch)
        far_q, far_k = parted(g_r[ch, :, :, 0:CW])
        out_q[:, cols] = (nq[:, cols] + far_q.astype(F32)).astype(BF16)
        out_k[:, cols] = (nk[:, cols] + far_k.astype(F32)).astype(BF16)
        far_low, far_high = parted(g_r[ch, :, :, CW:])
        out_v[:, low] = (nv[:, low] + far_low.astype(F32)).astype(BF16)
        out_v[:, high] = (nv[:, high] + far_high.astype(F32)).astype(BF16)

    for copy in ahead:
        copy.wait_recv()
    total = z_s[z].astype(F32)
    for step in range(NZ - 1):
        total = total + z_r[step].astype(F32)
    for n in range(CHUNKS):
        out_w[:, n * PAIR : (n + 1) * PAIR] = total[n * ROWS : (n + 1) * ROWS] * factor
    for copy in w_started + r_started:
        copy.wait_send()
    for ch in range(CH):
        departed(v_s.at[ch], A_O + ch)
        departed(qk_s.at[ch], A_G + ch)
        departed(l_s.at[ch], A_L + ch)
        departed(s_s.at[ch], A_S + ch)
    departed(go_s, A_GO)


def reorder(*refs):
    square = (TILES, TILES)
    line, lane = iota(square, 0), iota(square, 1)
    back = (lane == lax.rem(line, NS) * EACH + lax.div(line, NS)).astype(F32).astype(BF16)
    for src, dst in zip(refs[:4], refs[4:]):
        dst[...] = nn(back, src[...]).astype(BF16)


def natural(rows):
    wide = WIDTH // 2
    block = pl.BlockSpec((TILES, wide), lambda n: (0, n))
    return pl.pallas_call(
        reorder,
        grid=(WIDTH // wide,),
        out_shape=[jax.ShapeDtypeStruct((TILES, WIDTH), BF16)] * 4,
        in_specs=[block] * 4,
        out_specs=[block] * 4,
    )(*rows)


def layer(queries, key_rows, value_rows, tissue, segment_len, dilation, out_weight, grad_out):
    shape = (TILES, WIDTH)
    vmem = pl.BlockSpec(memory_space=pltpu.VMEM)
    smem = pl.BlockSpec(memory_space=pltpu.SMEM)
    low, wide = pltpu.VMEM(shape, BF16), pltpu.VMEM(shape, F32)
    stats = pltpu.VMEM((CH, NS, 1, PAIR), F32)
    table = pltpu.VMEM((PAIR, TILES), F32)
    square = pltpu.VMEM((TILES, TILES), jnp.int32)
    three = pltpu.VMEM((CH, NS, 2 * EACH, CW + HW), BF16)
    single = pltpu.VMEM((CH, NS, 2 * EACH, HW), BF16)
    ends = pltpu.VMEM((NS, 2 * EACH, WIDTH // 2), BF16)
    dma = pltpu.SemaphoreType.DMA
    factor = 1.0 / math.sqrt(NX * NC * NS * TILES)
    outs = pl.pallas_call(
        functools.partial(kernel, factor),
        out_shape=[jax.ShapeDtypeStruct(shape, BF16)] * 4 + [jax.ShapeDtypeStruct((ROWS, WIDTH), F32)],
        in_specs=[vmem] * 5 + [smem] * 2 + [vmem],
        out_specs=[vmem] * 5,
        scratch_shapes=[low] * 11 + [wide] + [low, pltpu.VMEM((WIDTH, TILES), BF16)] + [wide] * 3
        + [square] * 2 + [pltpu.VMEM((CH, TILES, PAIR), F32), pltpu.VMEM((CH, PAIR, TILES), F32), table]
        + [pltpu.VMEM((8, TILES), F32), pltpu.VMEM((TILES, TILES), F32)]
        + [three, single, three, single, three, ends, ends]
        + [stats] * 4
        + [
            pltpu.VMEM((16, WIDTH), BF16),
            pltpu.VMEM((PACK, PAIR), BF16),
            pltpu.VMEM((NZ, PACK, PAIR), BF16),
            pltpu.VMEM((WIDTH, WIDTH), BF16),
            pltpu.VMEM((NX, LINE, WIDTH), BF16),
            pltpu.VMEM((NX, LINE, WIDTH), BF16),
            pltpu.VMEM((LINE, WIDTH), F32),
            pltpu.VMEM((NX - 1, LINE, WIDTH), BF16),
            pltpu.VMEM((NX - 1, LINE, WIDTH), BF16),
            pltpu.VMEM((NY, BLOCK, WIDTH), F32),
            pltpu.VMEM((NY - 1, BLOCK, WIDTH), F32),
            pltpu.VMEM((NZ, PACK, PAIR), BF16),
            pltpu.VMEM((NZ - 1, PACK, PAIR), BF16),
            dma((A_ALL,)),
            dma((A_ALL,)),
            dma((NZ + NY + 2 * NX,)),
            dma((NZ,)),
            dma((NY,)),
            dma((NX,)),
            dma((NX,)),
            dma((NZ + NY + 2 * NX,)),
            dma((NX,)),
            dma((NX,)),
            dma((NY,)),
            dma((NZ,)),
        ],
        compiler_params=pltpu.CompilerParams(
            collective_id=0, has_side_effects=True, vmem_limit_bytes=60 * 1024 * 1024
        ),
    )(
        queries[0], key_rows[0], value_rows[0], grad_out[0], tissue, segment_len, dilation, out_weight
    )
    return tuple(out[None] for out in natural(outs[:4])) + (outs[4],)


def solution(mesh):
    tiles = P("slide", "seq", None)
    rows = P(("slide", "seq"), None)
    return jax.shard_map(
        layer,
        mesh=mesh,
        in_specs=(tiles, tiles, tiles, P("slide", "seq"), P(), P(), rows, tiles),
        out_specs=(tiles, tiles, tiles, tiles, rows),
        check_vma=False,
    )
```

```python
import functools
import math

import jax
import jax.numpy as jnp
from jax import lax
from jax.experimental import pallas as pl
from jax.experimental.pallas import tpu as pltpu
from jax.sharding import PartitionSpec as P

HD = 64
PAIR = 2 * HD
NX, NC, NY, NZ = 4, 2, 4, 8
NS = NY * NZ
TILES = 256
WIDTH = 1536
EACH = TILES // NS
PAIRS = WIDTH // PAIR
CH = 3
CW = WIDTH // CH
HW = CW // 2
CP = PAIRS // CH
LINE = WIDTH // (NX * NC)
BLOCK = LINE // NY
ROWS = BLOCK // NZ
CHUNKS = WIDTH // PAIR
PACK = 80
FLAG = 100.0
LOG2E = 1.4426950408889634
SCALE = HD**-0.5
NONE = -1e30
FLOOR = -1e29
MESH = pl.DeviceIdType.MESH
F32 = jnp.float32
BF16 = jnp.bfloat16
A_QK, A_V, A_O, A_G, A_GV, A_L, A_S = (CH * n for n in range(7))
A_GO = 7 * CH
A_ALL = 7 * CH + 1
SLOTS = PAIR // EACH


def nt(a, b):
    return lax.dot_general(a, b, (((1,), (1,)), ((), ())), preferred_element_type=F32)


def nn(a, b):
    return lax.dot_general(a, b, (((1,), (0,)), ((), ())), preferred_element_type=F32)


def tn(a, b):
    return lax.dot_general(a, b, (((0,), (0,)), ((), ())), preferred_element_type=F32)


def doubled(value):
    high = value.astype(BF16)
    return jnp.concatenate([high, (value - high.astype(F32)).astype(BF16)], axis=1)


def tripled(value):
    high = value.astype(BF16)
    rest = value - high.astype(F32)
    middle = rest.astype(BF16)
    return jnp.concatenate([high, middle, (rest - middle.astype(F32)).astype(BF16)], axis=1)


def slot_lane(lane):
    slot = lax.rem(lane, SLOTS)
    inner = lax.rem(slot, SLOTS // 2)
    return lax.div(inner, 2) + HD * lax.rem(inner, 2) + 16 * lax.div(slot, SLOTS // 2)


def own_slots():
    shape = (TILES, PAIR)
    return lax.div(iota(shape, 1), SLOTS) == lax.rem(iota(shape, 0), EACH)


def folded(stats):
    tall = (3 * PAIR, PAIR)
    move = (lax.rem(iota(tall, 0), PAIR) == slot_lane(iota(tall, 1))).astype(F32).astype(BF16)
    spread = jnp.where(own_slots(), nn(tripled(stats), move), 0.0)
    return jnp.sum(spread.reshape(NS, EACH, PAIR), axis=1, keepdims=True)


def unfolded(rows):
    tall = (3 * PAIR, PAIR)
    move = (slot_lane(lax.rem(iota(tall, 0), PAIR)) == iota(tall, 1)).astype(F32).astype(BF16)
    spread = jnp.broadcast_to(rows, (NS, EACH, PAIR)).reshape(TILES, PAIR)
    return nn(tripled(jnp.where(own_slots(), spread, 0.0)), move)


def iota(shape, axis):
    return lax.broadcasted_iota(jnp.int32, shape, axis)


def halves():
    low = (iota((1, PAIR), 1) < HD).astype(F32)
    return low.astype(BF16), (1.0 - low).astype(BF16)


def joined(a, b):
    shape = (NS, EACH, a.shape[1])
    both = [a.astype(F32).reshape(shape), b.astype(F32).reshape(shape)]
    return jnp.concatenate(both, axis=1).astype(BF16)


def parted(block):
    wide = block.astype(F32)
    shape = (TILES, block.shape[2])
    return wide[:, :EACH].reshape(shape).astype(BF16), wide[:, EACH:].reshape(shape).astype(BF16)


def unfold():
    line = iota((CHUNKS * BLOCK, PAIR), 0)
    inner = lax.rem(line, BLOCK)
    want = lax.div(inner, ROWS) * PACK + lax.div(line, BLOCK) * ROWS + lax.rem(inner, ROWS)
    lane = iota((CHUNKS * BLOCK, PAIR), 1)
    parts = [(lane + PAIR * n == want).astype(F32).astype(BF16) for n in range(NZ * PACK // PAIR)]
    return jnp.concatenate(parts, axis=1)


def stacked(value):
    return jnp.concatenate([value[:, n * PAIR : (n + 1) * PAIR] for n in range(CHUNKS)], axis=0)


def pair_at(p):
    return pl.ds(pl.multiple_of(p * PAIR, PAIR), PAIR)


def forward_pair(q, k, v, masked):
    ones = halves()
    tops, sums = [], []
    for e in range(2):
        scores = masked(e, nt(q * ones[e], k) * (SCALE * LOG2E))
        top = jnp.maximum(jnp.max(scores, axis=1, keepdims=True), FLOOR)
        weights = jnp.exp2(scores - top).astype(BF16)
        tops.append(top)
        sums.append(nn(weights, v * ones[e] + ones[1 - e]))
    low = iota((TILES, PAIR), 1) < HD
    total = pltpu.roll(jnp.where(low, sums[1], sums[0]), HD, 1)
    total = jnp.maximum(total, 1e-30)
    out = jnp.where(low, sums[0], sums[1]) / total
    lse = jnp.where(low, tops[0], tops[1]) + jnp.log(total) * LOG2E
    return out, lse


def backward_pair(q, k, v, d, masked, lse, delta):
    ones = halves()
    gq = gk = gv = None
    for e in range(2):
        qe, de, ke = q * ones[e], d * ones[e], k * ones[e]
        probs = masked(e, nt(k, qe) * (SCALE * LOG2E) - lse[e])
        dscore = (probs * (nt(v, de) - delta[e])).astype(BF16)
        terms = (tn(dscore, ke), nn(dscore, qe), nn(probs.astype(BF16), de))
        gq, gk, gv = terms if e == 0 else (gq + terms[0], gk + terms[1], gv + terms[2])
    return gq * SCALE, gk * SCALE, gv


def remote(src, dst, send, recv, peer):
    return pltpu.make_async_remote_copy(
        src_ref=src, dst_ref=dst, send_sem=send, recv_sem=recv, device_id=peer, device_id_type=MESH
    )


def kernel(
    factor,
    q_in, k_in, v_in, g_in, keep_in, seg, dil, w_in,
    out_lo, out_q, out_k, out_v, out_w,
    qp, kp, vp, gp, dp, qf, kf, vf, gf, df, of, o_near, attn, attn_t, nq, nk, nv,
    x_fwd, x_bwd, stat, stat_t, far_t, bias_row, bias_col,
    qk_s, v_s, gv_s, qk_r, v_r, o_r, g_r, gv_r, go_s, go_r,
    l_s, l_r, s_s, s_r,
    w_pad, w_src, w_z, w_full,
    c_s, c_r, own, x_s, x_r, y_s, y_r, z_s, z_r,
    a_send, a_recv, w_send, wz_recv, wy_recv, wx_recv, wc_recv,
    r_send, rc_recv, rx_recv, ry_recv, rz_recv,
):
    slide = lax.axis_index("slide")
    me = lax.axis_index("seq")
    x, c = lax.div(slide, NC), lax.rem(slide, NC)
    y, z = lax.div(me, NZ), lax.rem(me, NZ)

    def device(xx, cc, yy, zz):
        return (xx * NC + cc, yy * NZ + zz)

    def peer_of(n):
        return lax.rem(y + lax.div(n, NZ), NY) * NZ + lax.rem(z + lax.rem(n, NZ), NZ)

    sibling = device(x, 1 - c, y, z)
    barrier = pltpu.get_barrier_semaphore()

    def greet(n, carry):
        pl.semaphore_signal(barrier, inc=1, device_id=(slide, peer_of(n)), device_id_type=MESH)
        return carry

    lax.fori_loop(1, NS, greet, 0)
    for peer in [sibling] + [device(lax.rem(x + step, NX), c, y, z) for step in range(1, NX)]:
        pl.semaphore_signal(barrier, inc=1, device_id=peer, device_id_type=MESH)

    def exchange(src, dst, k):
        def body(n, carry):
            peer = peer_of(n)
            remote(src.at[peer], dst.at[me], a_send.at[k], a_recv.at[k], (slide, peer)).start()
            return carry

        lax.fori_loop(1, NS, body, 0)
        dst.at[me][...] = src.at[me][...]

    def arrived(dst, k):
        part = dst.at[pl.ds(0, NS - 1)]
        pltpu.make_async_copy(part, part, a_recv.at[k]).wait()

    def departed(src, k):
        part = src.at[pl.ds(0, NS - 1)]
        pltpu.make_async_copy(part, part, a_send.at[k]).wait()

    w_started, r_started = [], []

    def send_w(src, dst, recv, peer):
        copy = remote(src, dst, w_send.at[len(w_started)], recv, peer)
        copy.start()
        w_started.append(copy)
        return copy

    def send_r(src, dst, recv, peer):
        copy = remote(src, dst, r_send.at[len(r_started)], recv, peer)
        copy.start()
        r_started.append(copy)
        return copy

    def line_of(xx, cc):
        return pl.ds(pl.multiple_of((xx * NC + cc) * LINE, 16), LINE)

    square = (TILES, TILES)
    line, lane = iota(square, 0), iota(square, 1)
    order = (lane == lax.rem(line, EACH) * NS + lax.div(line, EACH)).astype(F32).astype(BF16)
    keep = keep_in[...].astype(F32).astype(BF16)
    keep_cols = nt(order, jnp.broadcast_to(keep, (PAIR, TILES)))
    keep_wide = jnp.concatenate([keep_cols] * (CW // PAIR), axis=1) > 0.5
    for ch in range(CH):
        cols = pl.ds(ch * CW, CW)
        q = nn(order, q_in[:, cols])
        k = nn(order, k_in[:, cols])
        qk_s[ch] = joined(q, jnp.where(keep_wide, k, FLAG))
        if ch == 0:
            pl.semaphore_wait(barrier, NS - 1 + NX)
        if ch == 0:
            exchange(qk_s.at[ch], qk_r.at[ch], A_QK + ch)
            w_pad[...] = jnp.zeros_like(w_pad)
            w_pad[0:ROWS, :] = w_in[...]
            out_row, in_row = iota((PACK, CHUNKS * 16), 0), iota((PACK, CHUNKS * 16), 1)
            chosen = (lax.div(out_row, ROWS) == lax.div(in_row, 16)) & (lax.rem(out_row, ROWS) == lax.rem(in_row, 16))
            w_src[...] = nn(chosen.astype(F32).astype(BF16), stacked(w_pad[...])).astype(BF16)
            w_z[z] = w_src[...]
            wz = [
                send_w(w_src, w_z.at[z], wz_recv.at[step - 1], device(x, c, y, lax.rem(z + step, NZ)))
                for step in range(1, NZ)
            ]
        qp[:, cols] = q.astype(BF16)
        kp[:, cols] = k.astype(BF16)
        v = nn(order, v_in[:, cols])
        v_s[ch] = joined(v[:, :HW], v[:, HW:])
        if ch == 0:
            exchange(v_s.at[ch], v_r.at[ch], A_V + ch)
        vp[:, cols] = v.astype(BF16)
        if ch == 0:
            half = WIDTH // 2
            ends = []
            for cols in (pl.ds(0, half), pl.ds(half, half)):
                ends.append(nn(order, g_in[:, cols]))
                gp[:, cols] = ends[-1].astype(BF16)
            go_s[...] = joined(*ends)
            exchange(go_s, go_r, A_GO)

    keep_row = nt(jnp.broadcast_to(keep, (16, TILES)), order)[0:1]
    pos_l = lax.rem(line, EACH) * NS + lax.div(line, EACH)
    pos_c = lax.rem(lane, EACH) * NS + lax.div(lane, EACH)
    apart = lax.bitwise_xor(pos_l, pos_c)
    same = line == lane
    x_fwd[...] = jnp.where(same, 0, apart + jnp.where(keep_row > 0.5, 0, 65536))
    x_bwd[...] = jnp.where(same, 0, apart + jnp.where(keep_wide[:, :TILES], 0, 65536))

    def bits(p, e):
        head = 2 * p + e
        return 65536 + (TILES - seg[head]) + (dil[head] - 1)

    for copy in wz:
        copy.wait_recv()
    mine = pl.ds(pl.multiple_of(((x * NC + c) * NY + y) * BLOCK, 16), BLOCK)
    rows = nn(unfold(), w_z[...].reshape(NZ * PACK, PAIR)).astype(BF16)
    for n in range(CHUNKS):
        w_full[mine, n * PAIR : (n + 1) * PAIR] = rows[n * BLOCK : (n + 1) * BLOCK]
    wy = [
        send_w(w_full.at[mine], w_full.at[mine], wy_recv.at[step - 1], device(x, c, lax.rem(y + step, NY), z))
        for step in range(1, NY)
    ]

    def put_stat(p, stats, values):
        return jnp.where(lax.rem(iota((TILES, PAIR), 1), HD) == p, values, stats)

    def near_forward(ch, p, stats):
        at = pair_at(p)

        def masked(e, scores):
            return jnp.where(lax.bitwise_and(x_fwd[...], bits(p, e)) == 0, scores, NONE)

        out, lse = forward_pair(qp[:, at], kp[:, at], vp[:, at], masked)
        o_near[:, at] = out
        return put_stat(p - ch * CP, stats, lse)

    def near_chunk(ch):
        empty = jnp.zeros((TILES, PAIR), F32)
        stat[ch] = lax.fori_loop(ch * CP, (ch + 1) * CP, functools.partial(near_forward, ch), empty)

    def send_chunk(ch):
        exchange(qk_s.at[ch], qk_r.at[ch], A_QK + ch)
        exchange(v_s.at[ch], v_r.at[ch], A_V + ch)

    near_chunk(0)
    send_chunk(1)

    for copy in wy:
        copy.wait_recv()
    mine = line_of(x, c)
    wx = [
        send_w(w_full.at[mine], w_full.at[mine], wx_recv.at[step - 1], device(lax.rem(x + step, NX), c, y, z))
        for step in range(1, NX)
    ]
    wc = [send_w(w_full.at[mine], w_full.at[mine], wc_recv.at[0], sibling)]
    for ch in range(1, CH):
        near_chunk(ch)
    for ch in range(2, CH):
        send_chunk(ch)

    def columns(ch):
        return pl.ds(ch * CW, CW), pl.ds(ch * CW, HW), pl.ds(ch * CW + HW, HW)

    def far_forward(ch, p, stats):
        at = pair_at(p)
        out, lse = forward_pair(
            qf[:, at], kf[:, at], vf[:, at], lambda e, scores: scores + bias_row[0:1, :]
        )
        of[:, at] = out.astype(BF16)
        return put_stat(p - ch * CP, stats, lse)

    def far_chunk(ch):
        cols, low, high = columns(ch)
        arrived(qk_r.at[ch], A_QK + ch)
        qf[:, cols], kf[:, cols] = parted(qk_r[ch])
        if ch == 0:
            bias = jnp.where(kf[:, 0:PAIR].astype(F32) > FLAG / 2, NONE, 0.0)
            bias_col[...] = jnp.concatenate([bias, bias], axis=1)
            bias_row[...] = jnp.transpose(bias)[0:8]
        arrived(v_r.at[ch], A_V + ch)
        vf[:, low], vf[:, high] = parted(v_r[ch])
        empty = jnp.zeros((TILES, PAIR), F32)
        lse = lax.fori_loop(ch * CP, (ch + 1) * CP, functools.partial(far_forward, ch), empty)
        departed(v_s.at[ch], A_V + ch)
        v_s[ch] = joined(of[:, low], of[:, high])
        exchange(v_s.at[ch], o_r.at[ch], A_O + ch)
        l_s[ch] = folded(lse)
        exchange(l_s.at[ch], l_r.at[ch], A_L + ch)

    def combine(ch, share_near, share_far, p, delta):
        at = pair_at(p)
        near = p - ch * CP
        tall = (2 * PAIR, PAIR)
        first, second = lax.rem(iota(tall, 0), PAIR), iota(tall, 1)
        together = (first < HD) == (second < HD)
        spread = (together & (lax.rem(first, HD) == near)).astype(F32).astype(BF16)
        gather = (together & (lax.rem(second, HD) == near + 16)).astype(F32).astype(BF16)
        far = of[:, at].astype(F32)
        whole = nn(share_near, spread) * o_near[:, at] + nn(share_far, spread) * far
        attn[:, at] = whole.astype(BF16)
        attn_t[at, :] = jnp.transpose(whole).astype(BF16)
        return delta + nn(doubled(whole * dp[:, at].astype(F32)), gather)

    def combine_chunk(ch):
        cols, low, high = columns(ch)
        arrived(l_r.at[ch], A_L + ch)
        lse_near = stat[ch]
        lse_far = unfolded(l_r[ch])
        top = jnp.maximum(lse_near, lse_far)
        lse = top + jnp.log(jnp.exp2(lse_near - top) + jnp.exp2(lse_far - top)) * LOG2E
        share_near = doubled(jnp.exp2(lse_near - lse))
        share_far = doubled(jnp.exp2(lse_far - lse))
        arrived(o_r.at[ch], A_O + ch)
        of[:, low], of[:, high] = parted(o_r[ch])
        body = functools.partial(combine, ch, share_near, share_far)
        delta = lax.fori_loop(ch * CP, (ch + 1) * CP, body, jnp.zeros((TILES, PAIR), F32))
        stats = jnp.where(lax.rem(iota((TILES, PAIR), 1), HD) < 16, lse, delta)
        s_s[ch] = folded(stats)
        exchange(s_s.at[ch], s_r.at[ch], A_S + ch)
        stat_t[ch] = jnp.transpose(stats)

    def rows_of(table, p):
        lse = [table[pl.ds(p + HD * e, 1), :] for e in range(2)]
        delta = [table[pl.ds(p + HD * e + 16, 1), :] for e in range(2)]
        return lse, delta

    def far_backward(ch, p, carry):
        at = pair_at(p)
        here = pair_at(p - ch * CP)
        gq, gk, gv = backward_pair(
            qf[:, at], kf[:, at], vf[:, at], df[:, at],
            lambda e, scores: jnp.exp2(scores + bias_col[...]), *rows_of(far_t, p - ch * CP),
        )
        qk_s[ch, :, :, here] = joined(gq, gk)
        vf[:, at] = gv.astype(BF16)
        return carry

    def back_chunk(ch):
        cols, low, high = columns(ch)
        arrived(s_r.at[ch], A_S + ch)
        far_t[...] = jnp.transpose(unfolded(s_r[ch]))
        departed(qk_s.at[ch], A_QK + ch)
        lax.fori_loop(ch * CP, (ch + 1) * CP, functools.partial(far_backward, ch), 0)
        exchange(qk_s.at[ch], g_r.at[ch], A_G + ch)
        gv_s[ch] = joined(vf[:, low], vf[:, high])
        exchange(gv_s.at[ch], gv_r.at[ch], A_GV + ch)

    far_chunk(0)
    for step in range(1, NX):
        wx[step - 1].wait_recv()
        there = line_of(lax.rem(x + NX - step, NX), c)
        wc.append(send_w(w_full.at[there], w_full.at[there], wc_recv.at[step], sibling))
    for copy in wc:
        copy.wait_recv()
    arrived(go_r, A_GO)
    gf[:, : WIDTH // 2], gf[:, WIDTH // 2 :] = parted(go_r[...])
    for ch in range(CH):
        cols = pl.ds(ch * CW, CW)
        dp[:, cols] = nt(gp[...], w_full[cols, :]).astype(BF16)
        df[:, cols] = nt(gf[...], w_full[cols, :]).astype(BF16)
    for ch in range(1, CH):
        far_chunk(ch)
        combine_chunk(ch - 1)
    back_chunk(0)
    combine_chunk(CH - 1)

    for step in range(NX):
        to = lax.rem(x + step + 1, NX)
        c_s[step] = nn(attn_t[line_of(to, 1 - c), :], gp[...]).astype(BF16)
        send_r(c_s.at[step], c_r.at[step], rc_recv.at[step], sibling)
    for ch in range(1, CH - 1):
        back_chunk(ch)

    ahead = []
    for step in range(NX):
        to = lax.rem(x + step + 1, NX)
        r_started[step].wait_recv()
        total = nn(attn_t[line_of(to, c), :], gp[...]) + c_r[step].astype(F32)
        if step < NX - 1:
            x_s[step] = total.astype(BF16)
            ahead.append(send_r(x_s.at[step], x_r.at[step], rx_recv.at[step], device(to, c, y, z)))
        else:
            own[...] = total
    back_chunk(CH - 1)

    def near_backward(ch, p, carry):
        at = pair_at(p)

        def masked(e, scores):
            return jnp.where(lax.bitwise_and(x_bwd[...], bits(p, e)) == 0, jnp.exp2(scores), 0.0)

        nq[:, at], nk[:, at], nv[:, at] = backward_pair(
            qp[:, at], kp[:, at], vp[:, at], dp[:, at], masked, *rows_of(stat_t.at[ch], p - ch * CP)
        )
        return carry

    def near_back_chunk(ch):
        lax.fori_loop(ch * CP, (ch + 1) * CP, functools.partial(near_backward, ch), 0)

    near_back_chunk(0)
    for copy in ahead:
        copy.wait_recv()
    total = own[...]
    for step in range(NX - 1):
        total = total + x_r[step].astype(F32)
    y_s[...] = total.reshape(NY, BLOCK, WIDTH).astype(BF16)
    ahead = []
    for step in range(NY - 1):
        to = lax.rem(y + step + 1, NY)
        ahead.append(send_r(y_s.at[to], y_r.at[step], ry_recv.at[step], device(x, c, to, z)))
    for ch in range(1, CH):
        near_back_chunk(ch)
    for copy in ahead:
        copy.wait_recv()
    total = y_s[y].astype(F32)
    for step in range(NY - 1):
        total = total + y_r[step].astype(F32)
    z_s[...] = tn(unfold(), stacked(total).astype(BF16)).astype(BF16).reshape(NZ, PACK, PAIR)
    ahead = []
    for step in range(NZ - 1):
        to = lax.rem(z + step + 1, NZ)
        ahead.append(send_r(z_s.at[to], z_r.at[step], rz_recv.at[step], device(x, c, y, to)))

    for ch in range(CH):
        cols = pl.ds(ch * CW, CW)
        done = nn(attn[...], w_full[:, cols]).astype(BF16)
        out_lo[:, cols] = done

    for ch in range(CH):
        cols, low, high = pl.ds(ch * CW, CW), pl.ds(ch * CW, HW), pl.ds(ch * CW + HW, HW)
        arrived(g_r.at[ch], A_G + ch)
        far_q, far_k = parted(g_r[ch])
        out_q[:, cols] = (nq[:, cols] + far_q.astype(F32)).astype(BF16)
        out_k[:, cols] = (nk[:, cols] + far_k.astype(F32)).astype(BF16)
        arrived(gv_r.at[ch], A_GV + ch)
        far_low, far_high = parted(gv_r[ch])
        out_v[:, low] = (nv[:, low] + far_low.astype(F32)).astype(BF16)
        out_v[:, high] = (nv[:, high] + far_high.astype(F32)).astype(BF16)

    for copy in ahead:
        copy.wait_recv()
    total = z_s[z].astype(F32)
    for step in range(NZ - 1):
        total = total + z_r[step].astype(F32)
    for n in range(CHUNKS):
        out_w[:, n * PAIR : (n + 1) * PAIR] = total[n * ROWS : (n + 1) * ROWS] * factor
    for copy in w_started + r_started:
        copy.wait_send()
    for ch in range(CH):
        departed(v_s.at[ch], A_O + ch)
        departed(qk_s.at[ch], A_G + ch)
        departed(gv_s.at[ch], A_GV + ch)
        departed(l_s.at[ch], A_L + ch)
        departed(s_s.at[ch], A_S + ch)
    departed(go_s, A_GO)


def reorder(*refs):
    square = (TILES, TILES)
    line, lane = iota(square, 0), iota(square, 1)
    back = (lane == lax.rem(line, NS) * EACH + lax.div(line, NS)).astype(F32).astype(BF16)
    for src, dst in zip(refs[:4], refs[4:]):
        dst[...] = nn(back, src[...]).astype(BF16)


def natural(rows):
    wide = WIDTH // 2
    block = pl.BlockSpec((TILES, wide), lambda n: (0, n))
    return pl.pallas_call(
        reorder,
        grid=(WIDTH // wide,),
        out_shape=[jax.ShapeDtypeStruct((TILES, WIDTH), BF16)] * 4,
        in_specs=[block] * 4,
        out_specs=[block] * 4,
    )(*rows)


def layer(queries, key_rows, value_rows, tissue, segment_len, dilation, out_weight, grad_out):
    shape = (TILES, WIDTH)
    vmem = pl.BlockSpec(memory_space=pltpu.VMEM)
    smem = pl.BlockSpec(memory_space=pltpu.SMEM)
    low, wide = pltpu.VMEM(shape, BF16), pltpu.VMEM(shape, F32)
    stats = pltpu.VMEM((CH, NS, 1, PAIR), F32)
    table = pltpu.VMEM((PAIR, TILES), F32)
    square = pltpu.VMEM((TILES, TILES), jnp.int32)
    both = pltpu.VMEM((CH, NS, 2 * EACH, CW), BF16)
    single = pltpu.VMEM((CH, NS, 2 * EACH, HW), BF16)
    ends = pltpu.VMEM((NS, 2 * EACH, WIDTH // 2), BF16)
    dma = pltpu.SemaphoreType.DMA
    factor = 1.0 / math.sqrt(NX * NC * NS * TILES)
    outs = pl.pallas_call(
        functools.partial(kernel, factor),
        out_shape=[jax.ShapeDtypeStruct(shape, BF16)] * 4 + [jax.ShapeDtypeStruct((ROWS, WIDTH), F32)],
        in_specs=[vmem] * 5 + [smem] * 2 + [vmem],
        out_specs=[vmem] * 5,
        scratch_shapes=[low] * 11 + [wide] + [low, pltpu.VMEM((WIDTH, TILES), BF16)] + [wide] * 3
        + [square] * 2 + [pltpu.VMEM((CH, TILES, PAIR), F32), pltpu.VMEM((CH, PAIR, TILES), F32), table]
        + [pltpu.VMEM((8, TILES), F32), pltpu.VMEM((TILES, TILES), F32)]
        + [both, single, single, both, single, single, both, single, ends, ends]
        + [stats] * 4
        + [
            pltpu.VMEM((16, WIDTH), BF16),
            pltpu.VMEM((PACK, PAIR), BF16),
            pltpu.VMEM((NZ, PACK, PAIR), BF16),
            pltpu.VMEM((WIDTH, WIDTH), BF16),
            pltpu.VMEM((NX, LINE, WIDTH), BF16),
            pltpu.VMEM((NX, LINE, WIDTH), BF16),
            pltpu.VMEM((LINE, WIDTH), F32),
            pltpu.VMEM((NX - 1, LINE, WIDTH), BF16),
            pltpu.VMEM((NX - 1, LINE, WIDTH), BF16),
            pltpu.VMEM((NY, BLOCK, WIDTH), BF16),
            pltpu.VMEM((NY - 1, BLOCK, WIDTH), BF16),
            pltpu.VMEM((NZ, PACK, PAIR), BF16),
            pltpu.VMEM((NZ - 1, PACK, PAIR), BF16),
            dma((A_ALL,)),
            dma((A_ALL,)),
            dma((NZ + NY + 2 * NX,)),
            dma((NZ,)),
            dma((NY,)),
            dma((NX,)),
            dma((NX,)),
            dma((NZ + NY + 2 * NX,)),
            dma((NX,)),
            dma((NX,)),
            dma((NY,)),
            dma((NZ,)),
        ],
        compiler_params=pltpu.CompilerParams(
            collective_id=0, has_side_effects=True, vmem_limit_bytes=60 * 1024 * 1024
        ),
    )(
        queries[0], key_rows[0], value_rows[0], grad_out[0], tissue, segment_len, dilation, out_weight
    )
    return tuple(out[None] for out in natural(outs[:4])) + (outs[4],)


def solution(mesh):
    tiles = P("slide", "seq", None)
    rows = P(("slide", "seq"), None)
    return jax.shard_map(
        layer,
        mesh=mesh,
        in_specs=(tiles, tiles, tiles, P("slide", "seq"), P(), P(), rows, tiles),
        out_specs=(tiles, tiles, tiles, tiles, rows),
        check_vma=False,
    )
```
